32 devices in a mesh: dp: 4 (over x, core), cp: 8 (over z, y).
Axes of the slice: x: 2, y: 2, z: 4, core: 2. Of those that a mesh axis runs over, the one named last changes fastest.
Arguments:
- q_raw: bfloat16 [4096, 4096], P(('dp', 'cp')), may hold values from -60 to 60
- k_raw: bfloat16 [4096, 512], P(('dp', 'cp')), may hold values from -60 to 60
- values: bfloat16 [4096, 512], P(('dp', 'cp')), may hold values from -6 to 6
- loss_grad: bfloat16 [4096, 4096], P(('dp', 'cp')), may hold values from -6 to 6
- send_order: int32 [32, 128], P(('dp', 'cp')), may hold values from 0 to 127, each once within a row
- doc_blocks: int32 [4, 8], P('dp', 'cp'), may hold values from 0 to 2, never falling along the last dimension, each value on 1 to 5 neighbouring positions
- gain_q: float32 [128], replicated, may hold values from 0.6 to 4.6
- gain_k: float32 [128], replicated, may hold values from 0.6 to 4.6
Outputs:
- attn_out: bfloat16 [4096, 4096], P(('dp', 'cp'))
- dq_raw: bfloat16 [4096, 4096], P(('dp', 'cp'))
- dk_raw: bfloat16 [4096, 512], P(('dp', 'cp'))
- dv_out: bfloat16 [4096, 512], P(('dp', 'cp'))
- dgain_q: float32 [128], replicated
- dgain_k: float32 [128], replicated
The draws below stay inside these ranges and needn't reach their ends.
Inputs may be any that keep to these rules, and one draw needn't show every extreme that they name: `send_order`: each row is a permutation of 0 to 127. `doc_blocks`: within each row ids never fall, every id 0 to 2 occurs, each document covers 1 to 5 consecutive blocks, and some document covers exactly 5.
All inputs are finite; a program needn't handle non-finite values.
Results may differ from the reference program's by a relative error of at most 0.033.
The reference program's roundings to bfloat16 on the way count: a program that leaves them out, or rounds other values in their place, can miss the bound.
Values may be sent and summed in bfloat16 or wider, within the bound.
A program may use at most 128 MiB of HBM per device.

```python
import math
import jax
import jax.numpy as jnp
import numpy as np
from jax import lax

HEADS = 32
KV_HEADS = 4
D_HEAD = 128
BLOCK = 128
MOST_BLK = 5
TOK_DEV = 128
ROWS_PEER = 32
GROUP_BLK = 8
DOCS = 3
TOKENS = 4096
N_DP = 4
N_CP = 8


def shared_keys(key):
    return jnp.clip(jax.random.normal(key, (TOKENS, KV_HEADS, D_HEAD), jnp.float32), -6.0, 6.0)


def draw_k_raw(key, part):
    base = shared_keys(key)
    return base.reshape(TOKENS, KV_HEADS * D_HEAD).astype(jnp.bfloat16)


def draw_q_raw(key, part):
    key = jax.random.fold_in(key, 3)
    fresh = jnp.clip(jax.random.normal(key, (TOKENS, HEADS, D_HEAD), jnp.float32), -6.0, 6.0)
    return fresh.reshape(TOKENS, HEADS * D_HEAD).astype(jnp.bfloat16)


def draw_gain_q(key, part):
    key = jax.random.fold_in(key, 11)
    return jax.random.uniform(key, (D_HEAD,), jnp.float32, 0.6, 1.6)


def draw_gain_k(key, part):
    key = jax.random.fold_in(key, 13)
    return jax.random.uniform(key, (D_HEAD,), jnp.float32, 0.6, 1.6)


def levels(key, shape, split, least, top_value):
    loudness, own = 1.0, jax.random.fold_in(key, 6)
    for dim, shards_of in split:
        steps = jnp.exp(jax.random.uniform(jax.random.fold_in(own, dim), (shards_of,), jnp.float32, least / len(split), top_value / len(split)))
        loudness = loudness * jnp.repeat(steps, shape[dim] // shards_of).reshape([-1 if axis == dim else 1 for axis in range(len(shape))])
    return loudness


def split_up(number_of, total, bound, slope):
    weights = [(1 << 20) // math.isqrt(grade ** slope) + 1 for grade in range(2, number_of + 1)]
    surplus, counts = total - bound - (number_of - 1), [1] * (number_of - 1)
    while surplus > 0:
        movable = [i for i in range(number_of - 1) if counts[i] < bound]
        whole, left = sum([weights[i] for i in movable]), surplus
        for i in movable:
            extra = min(bound - counts[i], max(1, left * weights[i] // whole), surplus)
            counts[i] = counts[i] + extra
            surplus = surplus - extra
    return np.array([bound] + counts)


def ragged(stream_key, number_of, total, limit, lean):
    if number_of == 2:
        one = jax.random.randint(stream_key, (), max(1, total - limit), min(limit, total - 1) + 1)
        return jnp.stack([one, total - one])
    tallies = jnp.asarray(split_up(number_of, total, limit, lean), jnp.int32)
    pairs = (number_of - 1) // 2
    source_of, sink = tallies[1:1 + 2 * pairs:2], tallies[2:2 + 2 * pairs:2]
    margin = jnp.minimum(source_of - 1, limit - sink)
    shifted = jax.random.randint(jax.random.fold_in(stream_key, 1), (pairs,), 0, 1 << 20) % (margin + 1)
    tallies = tallies.at[1:1 + 2 * pairs:2].set(source_of - shifted).at[2:2 + 2 * pairs:2].set(sink + shifted)
    return tallies[jax.random.permutation(jax.random.fold_in(stream_key, 2), number_of)]


def gaussian(stream_key, shape, width, bound, cuts=(), held_as=jnp.bfloat16):
    entries = jax.random.normal(stream_key, shape, jnp.float32) * width
    if len(cuts) > 0:
        entries = levels(stream_key, shape, cuts, -0.22, 0.18) * entries
    return jnp.clip(entries, min=-bound, max=bound).astype(held_as)


def setup_inputs(seed: int = 0) -> dict:
    keys = jax.random.split(jax.random.key(seed), 9)
    return {
        "q_raw": draw_q_raw(jax.random.fold_in(keys[8], 71), 0),
        "k_raw": draw_k_raw(jax.random.fold_in(keys[8], 71), 0),
        "values": gaussian(keys[2], (TOKENS, KV_HEADS * D_HEAD), 1.0, 6.0, ((0, 32),)),
        "loss_grad": gaussian(keys[3], (TOKENS, HEADS * D_HEAD), 1.0, 6.0, ((0, 32),)),
        "send_order": jax.vmap(lambda own: jax.random.permutation(own, TOK_DEV))(jax.random.split(keys[4], (N_DP * N_CP))).reshape((N_DP * N_CP, TOK_DEV)).astype(jnp.int32),
        "doc_blocks": jax.vmap(lambda own: jnp.searchsorted(jnp.cumsum(ragged(own, DOCS, GROUP_BLK, MOST_BLK, 2)), jnp.arange(GROUP_BLK), side="right"))(jax.random.split(keys[5], N_DP)).reshape((N_DP, GROUP_BLK)).astype(jnp.int32),
        "gain_q": draw_gain_q(jax.random.fold_in(keys[8], 71), 0),
        "gain_k": draw_gain_k(jax.random.fold_in(keys[8], 71), 0),
    }


EPSILON = 1e-06
THETA = 1000000.0
NEGATIVE = -1e+30

def normalize(raw_rows, gain_vec, head_count):
    values_f = raw_rows.astype(jnp.float32).reshape(raw_rows.shape[0], head_count, -1)
    inv_norm = lax.rsqrt(lax.optimization_barrier(jnp.mean(values_f * values_f, axis=-1, keepdims=True)) + EPSILON)
    unit_vec = values_f * inv_norm
    return (unit_vec, inv_norm, unit_vec * gain_vec)

def rope_tables(position, head_dim):
    half_dim = head_dim // 2
    frequency = THETA ** (-(jnp.arange(half_dim, dtype=jnp.float32) * 2.0 / head_dim))
    angles = position.astype(jnp.float32)[:, None] * frequency[None, :]
    return (jnp.cos(angles)[:, None, :], jnp.sin(angles)[:, None, :])

def rotate(vectors, cosine, sine_tab):
    half_dim = vectors.shape[-1] // 2
    leading = vectors[..., :half_dim]
    trailing = vectors[..., half_dim:]
    return jnp.concatenate([leading * cosine - trailing * sine_tab, trailing * cosine + leading * sine_tab], axis=-1)

def unrotate(cotangent, cosine, sine_tab):
    half_dim = cotangent.shape[-1] // 2
    leading = cotangent[..., :half_dim]
    trailing = cotangent[..., half_dim:]
    return jnp.concatenate([leading * cosine + trailing * sine_tab, trailing * cosine - leading * sine_tab], axis=-1)

def norm_back(cotangent, unit_vec, inv_norm, gain_vec):
    scaled_grad = cotangent * gain_vec
    inner_sum = lax.optimization_barrier(jnp.mean(scaled_grad * unit_vec, axis=-1, keepdims=True))
    return (inv_norm * (scaled_grad - unit_vec * inner_sum), lax.optimization_barrier(jnp.sum(cotangent * unit_vec, axis=(0, 1))))

def group_pass(group, q_raw, k_raw, values, loss_grad, send_order, doc_blocks, gain_q, gain_k):
    seq_len = N_CP * TOK_DEV
    group_size = HEADS // KV_HEADS
    inv_root = 1.0 / math.sqrt(D_HEAD)
    route = send_order.reshape(N_DP, N_CP, TOK_DEV)
    columns = lax.dynamic_slice_in_dim(route, group * ROWS_PEER, ROWS_PEER, 2)
    source_a = jnp.arange(N_DP, dtype=jnp.int32)[:, None, None]
    source_c = jnp.arange(N_CP, dtype=jnp.int32)[None, :, None]

    def pick(array):
        shaped = array.reshape(N_DP, N_CP, TOK_DEV, array.shape[1])
        taken = shaped[source_a, source_c, columns]
        return jnp.transpose(taken, (1, 0, 2, 3)).reshape(seq_len, array.shape[1])
    q_rows = pick(q_raw)
    k_rows = pick(k_raw)
    v_rows = pick(values)
    g_rows = pick(loss_grad)
    doc_ids = doc_blocks[group]
    first_block = lax.optimization_barrier(jnp.sum((doc_ids[None, :] < doc_ids[:, None]).astype(jnp.int32), axis=1))
    position = jnp.arange(seq_len, dtype=jnp.int32) - jnp.repeat(first_block, BLOCK) * BLOCK
    cosine, sine_tab = rope_tables(position, D_HEAD)
    q_unit, q_norm, q_scaled = normalize(q_rows, gain_q, HEADS)
    k_unit, k_norm, k_scaled = normalize(k_rows, gain_k, KV_HEADS)
    queries = rotate(q_scaled, cosine, sine_tab).astype(jnp.bfloat16).reshape(seq_len, KV_HEADS, group_size, D_HEAD)
    keys_rot = rotate(k_scaled, cosine, sine_tab).astype(jnp.bfloat16)
    values_kv = v_rows.reshape(seq_len, KV_HEADS, D_HEAD)
    g_heads = g_rows.reshape(seq_len, KV_HEADS, group_size, D_HEAD)
    stat_shape = (KV_HEADS, group_size, BLOCK)

    def block_pass(carried, block_idx):
        dk_acc, dv_acc = carried
        q_block = lax.dynamic_slice_in_dim(queries, block_idx * BLOCK, BLOCK, 0).astype(jnp.float32)
        g_block = lax.dynamic_slice_in_dim(g_heads, block_idx * BLOCK, BLOCK, 0).astype(jnp.float32)
        query_index = block_idx * BLOCK + jnp.arange(BLOCK, dtype=jnp.int32)

        def key_side(distance):
            key_block = block_idx - distance.astype(jnp.int32)
            active = (key_block >= 0) & (doc_ids[jnp.maximum(key_block, 0)] == doc_ids[block_idx])
            offset = jnp.maximum(key_block, 0) * BLOCK
            key_index = key_block * BLOCK + jnp.arange(BLOCK, dtype=jnp.int32)
            allowed = key_index[None, :] <= query_index[:, None]
            return (active, offset, allowed)

        def scores_at(offset):
            keys_block = lax.dynamic_slice_in_dim(keys_rot, offset, BLOCK, 0).astype(jnp.float32)
            return jnp.einsum('tkgd,ukd->kgtu', q_block, keys_block) * inv_root

        def max_step(distance, row_max):
            active, offset, allowed = key_side(distance)

            def taken(operands):
                scores = scores_at(operands[0])
                return lax.optimization_barrier(jnp.max(jnp.where(operands[1][None, None], scores, NEGATIVE), axis=-1))

            def skipped(operands):
                return jnp.full(stat_shape, NEGATIVE, jnp.float32)
            return jnp.maximum(row_max, lax.cond(active, taken, skipped, (offset, allowed)))
        row_max = lax.fori_loop(0, MOST_BLK, max_step, jnp.full(stat_shape, NEGATIVE, jnp.float32))

        def sum_step(distance, state):
            row_sum, out_acc = state
            active, offset, allowed = key_side(distance)

            def taken(operands):
                scores = scores_at(operands[0])
                weights = jnp.where(operands[1][None, None], jnp.exp(scores - row_max[..., None]), 0.0)
                values_block = lax.dynamic_slice_in_dim(values_kv, operands[0], BLOCK, 0).astype(jnp.float32)
                rounded = weights.astype(jnp.bfloat16).astype(jnp.float32)
                return (lax.optimization_barrier(jnp.sum(weights, axis=-1)), jnp.einsum('kgtu,ukd->tkgd', rounded, values_block))

            def skipped(operands):
                return (jnp.zeros(stat_shape, jnp.float32), jnp.zeros((BLOCK, KV_HEADS, group_size, D_HEAD), jnp.float32))
            add_sum, add_out = lax.cond(active, taken, skipped, (offset, allowed))
            return (row_sum + add_sum, out_acc + add_out)
        row_sum, out_acc = lax.fori_loop(0, MOST_BLK, sum_step, (jnp.zeros(stat_shape, jnp.float32), jnp.zeros((BLOCK, KV_HEADS, group_size, D_HEAD), jnp.float32)))
        out_block = (out_acc / jnp.transpose(row_sum, (2, 0, 1))[..., None]).astype(jnp.bfloat16)
        lse_row = row_max + jnp.log(row_sum)
        delta_row = jnp.transpose(lax.optimization_barrier(jnp.sum(g_block * out_block.astype(jnp.float32), axis=-1)), (1, 2, 0))

        def back_step(distance, state):
            dq_acc, dk_run, dv_run = state
            active, offset, allowed = key_side(distance)

            def taken(operands):
                scores = scores_at(operands[0])
                keys_block = lax.dynamic_slice_in_dim(keys_rot, operands[0], BLOCK, 0).astype(jnp.float32)
                values_block = lax.dynamic_slice_in_dim(values_kv, operands[0], BLOCK, 0).astype(jnp.float32)
                probs = jnp.where(operands[1][None, None], jnp.exp(scores - lse_row[..., None]), 0.0)
                dprobs = jnp.einsum('tkgd,ukd->kgtu', g_block, values_block)
                dscores = (probs * (dprobs - delta_row[..., None])).astype(jnp.bfloat16).astype(jnp.float32)
                probs_b = probs.astype(jnp.bfloat16).astype(jnp.float32)
                dq_part = jnp.einsum('kgtu,ukd->tkgd', dscores, keys_block) * inv_root
                dk_part = jnp.einsum('kgtu,tkgd->ukd', dscores, q_block) * inv_root
                dv_part = jnp.einsum('kgtu,tkgd->ukd', probs_b, g_block)
                return (dq_part, dk_part, dv_part)

            def skipped(operands):
                return (jnp.zeros((BLOCK, KV_HEADS, group_size, D_HEAD), jnp.float32), jnp.zeros((BLOCK, KV_HEADS, D_HEAD), jnp.float32), jnp.zeros((BLOCK, KV_HEADS, D_HEAD), jnp.float32))
            dq_part, dk_part, dv_part = lax.cond(active, taken, skipped, (offset, allowed))
            dk_run = lax.dynamic_update_slice_in_dim(dk_run, lax.dynamic_slice_in_dim(dk_run, offset, BLOCK, 0) + dk_part, offset, 0)
            dv_run = lax.dynamic_update_slice_in_dim(dv_run, lax.dynamic_slice_in_dim(dv_run, offset, BLOCK, 0) + dv_part, offset, 0)
            return (dq_acc + dq_part, dk_run, dv_run)
        dq_block, dk_acc, dv_acc = lax.fori_loop(0, MOST_BLK, back_step, (jnp.zeros((BLOCK, KV_HEADS, group_size, D_HEAD), jnp.float32), dk_acc, dv_acc))
        return ((dk_acc, dv_acc), (out_block, dq_block))
    zeros_kv = jnp.zeros((seq_len, KV_HEADS, D_HEAD), jnp.float32)
    (dk_total, dv_total), (out_blocks, dq_blocks) = lax.scan(block_pass, (zeros_kv, zeros_kv), jnp.arange(GROUP_BLK, dtype=jnp.int32))
    attn_rows = out_blocks.reshape(seq_len, HEADS * D_HEAD)
    dq_rot = dq_blocks.reshape(seq_len, HEADS, D_HEAD)
    dq_rows, gq_part = norm_back(unrotate(dq_rot, cosine, sine_tab), q_unit, q_norm, gain_q)
    dk_rows, gk_part = norm_back(unrotate(dk_total, cosine, sine_tab), k_unit, k_norm, gain_k)
    return (attn_rows, dq_rows.astype(jnp.bfloat16).reshape(seq_len, HEADS * D_HEAD), dk_rows.astype(jnp.bfloat16).reshape(seq_len, KV_HEADS * D_HEAD), dv_total.astype(jnp.bfloat16).reshape(seq_len, KV_HEADS * D_HEAD), gq_part, gk_part)

def reference(q_raw, k_raw, values, loss_grad, send_order, doc_blocks, gain_q, gain_k):

    def one_group(group):
        return group_pass(group, q_raw, k_raw, values, loss_grad, send_order, doc_blocks, gain_q, gain_k)
    attn_rows, dq_rows, dk_rows, dv_rows, gq_parts, gk_parts = lax.map(one_group, jnp.arange(N_DP, dtype=jnp.int32))
    factor = 1.0 / math.sqrt(TOKENS)
    return (attn_rows.reshape(TOKENS, HEADS * D_HEAD), dq_rows.reshape(TOKENS, HEADS * D_HEAD), dk_rows.reshape(TOKENS, KV_HEADS * D_HEAD), dv_rows.reshape(TOKENS, KV_HEADS * D_HEAD), lax.optimization_barrier(jnp.sum(gq_parts, axis=0)) * factor, lax.optimization_barrier(jnp.sum(gk_parts, axis=0)) * factor)
```

```python
import functools
import math

import jax
import jax.numpy as jnp
import numpy as np
from jax import lax
from jax.experimental import pallas as pl
from jax.experimental.pallas import tpu as pltpu
from jax.sharding import PartitionSpec as P

MOST_BLK = 5
EPSILON = 1e-06
THETA = 1000000.0
NEGATIVE = -1e30
MESH = pl.DeviceIdType.MESH
F32 = jnp.float32
BF16 = jnp.bfloat16


def dot(a, b):
    return jnp.dot(a, b, preferred_element_type=F32)


def dot_nt(a, b):
    return lax.dot_general(a, b, (((1,), (1,)), ((), ())), preferred_element_type=F32)


def flip(x, d):
    parts = [x[:, i : i + d].T for i in range(0, x.shape[1], d)]
    return parts[0] if len(parts) == 1 else jnp.concatenate(parts, axis=1)


def wide(x, n):
    return x if n == 1 else jnp.concatenate([x] * n, axis=1)


def rotate(x, cos, sin):
    half = x.shape[0] // 2
    lead, trail = x[:half], x[half:]
    return jnp.concatenate([lead * cos - trail * sin, trail * cos + lead * sin], axis=0)


def unrotate(x, cos, sin):
    half = x.shape[0] // 2
    lead, trail = x[:half], x[half:]
    return jnp.concatenate([lead * cos + trail * sin, trail * cos - lead * sin], axis=0)


def unit_of(x):
    inv = lax.rsqrt(jnp.mean(x * x, axis=0, keepdims=True) + EPSILON)
    return x * inv, inv


def norm_back(cot, unit, inv, gain):
    scaled = cot * gain
    inner = jnp.mean(scaled * unit, axis=0, keepdims=True)
    return inv * (scaled - unit * inner)


def kernel(
    n_dp, n_cp, kv, grp, d, tok, pair,
    q_hbm, k_hbm, v_hbm, g_hbm, order_ref, doc_ref, gq_ref, gk_ref, table_ref,
    out_hbm, dq_hbm, dk_ref, dv_ref, gains_q_ref, gains_k_ref,
    q_in, k_in, v_in, g_in, hot, kv_send, kv_recv, qg_send, qg_recv,
    id_send, id_recv, ring_send, ring_recv, keys, vals, keys_t, vals_t,
    grad_send, grad_recv, dk_own, dv_own, dk_sum, dv_sum, k_unit, k_inv,
    cos_ref, sin_ref, gq_t, gk_t, tri, out_buf, dq_buf, acc_q, part, tot, dp_recv, cp_recv,
    in_sem, out_sem, kvs_sem, kvr_sem, qgs_sem, qgr_sem, ids_sem, idr_sem,
    rs_sem, rr_sem, gs_sem, gr_sem, ds_sem, dr_sem, cs_sem, cr_sem,
):
    a = lax.axis_index("dp")
    c = lax.axis_index("cp")
    reach = min(MOST_BLK - 1, n_cp - 1)
    blocks = reach + 1
    width = grp * d
    rows = tok // n_dp
    inv_root = 1.0 / math.sqrt(d)
    exp_scale = inv_root * math.log2(math.e)

    def columns(h, size):
        return pl.ds(pl.multiple_of(h * size, size), size)

    def in_copy(h, src, dst, which):
        return pltpu.make_async_copy(
            src.at[:, columns(h, width)], dst.at[:, columns(h, width)], in_sem.at[2 + which, h]
        )

    k_copy = pltpu.make_async_copy(k_hbm, k_in, in_sem.at[0, 0])
    v_copy = pltpu.make_async_copy(v_hbm, v_in, in_sem.at[1, 0])
    k_copy.start()
    v_copy.start()
    for h in range(kv):
        in_copy(h, q_hbm, q_in, 0).start()
        in_copy(h, g_hbm, g_in, 1).start()

    barrier = pltpu.get_barrier_semaphore()
    for r in range(1, n_dp):
        pl.semaphore_signal(
            barrier, inc=1, device_id={"dp": lax.rem(a + r, n_dp)}, device_id_type=MESH
        )

    def greet(r, carry):
        pl.semaphore_signal(
            barrier, inc=1, device_id={"cp": lax.rem(c + r, n_cp)}, device_id_type=MESH
        )
        return carry

    lax.fori_loop(1, n_cp, greet, 0)

    own_id = jnp.broadcast_to(doc_ref[...], (8, 128))
    id_send[...] = own_id
    order = jnp.broadcast_to(order_ref[...], (tok, tok)).astype(F32).T
    slot = lax.broadcasted_iota(jnp.int32, (tok, tok), 1)
    hot[...] = jnp.where(order == slot.astype(F32), 1.0, 0.0).astype(BF16)
    gq_t[...] = jnp.broadcast_to(gq_ref[...], (d, d)).T
    gk_t[...] = jnp.broadcast_to(gk_ref[...], (d, d)).T
    tri[...] = jnp.where(
        lax.broadcasted_iota(jnp.int32, (tok, tok), 0)
        <= lax.broadcasted_iota(jnp.int32, (tok, tok), 1),
        0.0,
        NEGATIVE,
    )
    acc_q[...] = jnp.zeros_like(acc_q)
    for s in range(1, blocks):

        @pl.when(c < s)
        def _():
            id_recv[s - 1] = jnp.zeros((8, 128), jnp.int32)
            for h in range(kv):
                ring_recv[h, s - 1] = jnp.zeros((tok, 2 * d), BF16)

        @pl.when(c + s >= n_cp)
        def _():
            for h in range(kv):
                grad_recv[h, s - 1] = jnp.zeros((tok, 2 * d), BF16)

    k_copy.wait()
    v_copy.wait()
    kw = kv * d
    kv_send[:, :kw] = dot(hot[...], k_in[...]).astype(BF16)
    kv_send[:, kw:] = dot(hot[...], v_in[...]).astype(BF16)
    mine = pl.ds(pl.multiple_of(a * rows, rows), rows)
    kv_recv[mine, :] = kv_send[mine, :]

    pl.semaphore_wait(barrier, n_dp - 1 + n_cp - 1)

    def kv_copy(r):
        peer = lax.rem(a + r, n_dp)
        return pltpu.make_async_remote_copy(
            src_ref=kv_send.at[pl.ds(pl.multiple_of(peer * rows, rows), rows), :],
            dst_ref=kv_recv.at[mine, :],
            send_sem=kvs_sem.at[r - 1],
            recv_sem=kvr_sem.at[r - 1],
            device_id={"dp": peer},
            device_id_type=MESH,
        )

    def qg_copy(h, r):
        peer = lax.rem(a + r, n_dp)
        return pltpu.make_async_remote_copy(
            src_ref=qg_send.at[h, pl.ds(pl.multiple_of(peer * rows, rows), rows), :],
            dst_ref=qg_recv.at[h, mine, :],
            send_sem=qgs_sem.at[h, r - 1],
            recv_sem=qgr_sem.at[h, r - 1],
            device_id={"dp": peer},
            device_id_type=MESH,
        )

    def id_copy(s):
        return pltpu.make_async_remote_copy(
            src_ref=id_send,
            dst_ref=id_recv.at[s - 1],
            send_sem=ids_sem.at[s - 1],
            recv_sem=idr_sem.at[s - 1],
            device_id={"cp": lax.rem(c + s, n_cp)},
            device_id_type=MESH,
        )

    def ring_copy(h, s):
        return pltpu.make_async_remote_copy(
            src_ref=ring_send.at[h],
            dst_ref=ring_recv.at[h, s - 1],
            send_sem=rs_sem.at[h, s - 1],
            recv_sem=rr_sem.at[h, s - 1],
            device_id={"cp": lax.rem(c + s, n_cp)},
            device_id_type=MESH,
        )

    def grad_copy(h, s):
        return pltpu.make_async_remote_copy(
            src_ref=grad_send.at[h, s - 1],
            dst_ref=grad_recv.at[h, s - 1],
            send_sem=gs_sem.at[h, s - 1],
            recv_sem=gr_sem.at[h, s - 1],
            device_id={"cp": lax.rem(c + n_cp - s, n_cp)},
            device_id_type=MESH,
        )

    for r in range(1, n_dp):
        kv_copy(r).start()
    for s in range(1, blocks):

        @pl.when(c + s < n_cp)
        def _():
            id_copy(s).start()

    def gather(h, carry):
        in_copy(h, q_hbm, q_in, 0).wait()
        in_copy(h, g_hbm, g_in, 1).wait()
        qg_send[h, :, :width] = dot(hot[...], q_in[:, columns(h, width)]).astype(BF16)
        qg_send[h, :, width:] = dot(hot[...], g_in[:, columns(h, width)]).astype(BF16)
        qg_recv[h, mine, :] = qg_send[h, mine, :]
        for r in range(1, n_dp):
            qg_copy(h, r).start()
        return carry

    lax.fori_loop(0, kv, gather, 0)

    for s in range(1, blocks):

        @pl.when(c >= s)
        def _():
            id_copy(s).wait_recv()

    before = jnp.zeros((1, 128), F32)
    away = []
    for s in range(1, blocks):
        here = (c >= s).astype(F32)
        same = jnp.where(id_recv[s - 1, 0:1, :] == own_id[0:1, :], here, 0.0)
        before = before + same
        away.append(wide((1.0 - same) * -NEGATIVE, pair))
    half = d // 2
    cos = jnp.zeros((half, tok), F32)
    sin = jnp.zeros((half, tok), F32)
    for s in range(MOST_BLK):
        hit = before == float(s)
        cos = cos + jnp.where(hit, table_ref[:half, s * tok : (s + 1) * tok], 0.0)
        sin = sin + jnp.where(hit, table_ref[half:, s * tok : (s + 1) * tok], 0.0)
    cos_ref[...] = cos
    sin_ref[...] = sin

    for r in range(1, n_dp):
        kv_copy(r).wait_recv()

    for h in range(kv):
        x = kv_recv[:, h * d : (h + 1) * d].astype(F32).T
        unit, inv = unit_of(x)
        k_unit[h] = unit
        k_inv[h] = jnp.broadcast_to(inv, (8, tok))
        turned = rotate(unit * gk_t[...], cos_ref[...], sin_ref[...])
        ring_send[h, :, :d] = turned.T.astype(BF16)
        ring_send[h, :, d:] = kv_recv[:, kw + h * d : kw + (h + 1) * d]
        for s in range(1, blocks):

            @pl.when(c + s < n_cp)
            def _():
                ring_copy(h, s).start()

    def out_copy(h, src, dst, which):
        return pltpu.make_async_copy(
            src.at[:, columns(h, width)], dst.at[:, columns(h, width)], out_sem.at[which, h]
        )

    span = pair * d

    def head(h, carry):
        for r in range(1, n_dp):
            qg_copy(h, r).wait_recv()
        for s in range(1, blocks):

            @pl.when(c >= s)
            def _():
                ring_copy(h, s).wait_recv()

        for s in range(blocks):
            both = ring_send[h] if s == 0 else ring_recv[h, s - 1]
            keys[s * tok : (s + 1) * tok, :] = both[:, :d]
            vals[s * tok : (s + 1) * tok, :] = both[:, d:]
            keys_t[:, s * tok : (s + 1) * tok] = both[:, :d].T
            vals_t[:, s * tok : (s + 1) * tok] = both[:, d:].T
        dk_own[...] = jnp.zeros_like(dk_own)
        dv_own[...] = jnp.zeros_like(dv_own)

        def some(j, carry):
            cos = wide(cos_ref[...], pair)
            sin = wide(sin_ref[...], pair)
            gain = wide(gq_t[...], pair)
            unit, inv = unit_of(flip(qg_recv[h, :, columns(j, span)].astype(F32), d))
            turned = rotate(unit * gain, cos, sin).astype(BF16)
            g_at = pl.ds(pl.multiple_of(width + j * span, span), span)
            g_t = flip(qg_recv[h, :, g_at], d)
            scores = dot(keys[...], turned)
            parts = [scores[s * tok : (s + 1) * tok] for s in range(blocks)]
            parts[0] = parts[0] + wide(tri[...], pair)
            top = jnp.max(parts[0], axis=0, keepdims=True)
            for s in range(1, blocks):
                top = jnp.maximum(top, jnp.max(parts[s], axis=0, keepdims=True) - away[s - 1])
            weights = [
                jnp.exp2((parts[s] - (top if s == 0 else top + away[s - 1])) * exp_scale)
                for s in range(blocks)
            ]
            weights = jnp.concatenate(weights, axis=0)
            inv_sum = 1.0 / jnp.sum(weights, axis=0, keepdims=True)
            out_t = (dot(vals_t[...], weights.astype(BF16)) * inv_sum).astype(BF16)
            delta = jnp.sum(g_t.astype(F32) * out_t.astype(F32), axis=0, keepdims=True)
            probs = weights * inv_sum
            dprobs = dot(vals[...], g_t)
            dscores = (probs * (dprobs - delta)).astype(BF16)
            dk_own[...] += dot_nt(dscores, turned)
            dv_own[...] += dot_nt(probs.astype(BF16), g_t)
            dqn = unrotate(dot(keys_t[...], dscores) * inv_root, cos, sin)
            term = dqn * unit
            acc_q[...] += sum(term[:, i * d : (i + 1) * d] for i in range(pair))
            at = pl.ds(pl.multiple_of(h * width + j * span, span), span)
            out_buf[:, at] = flip(out_t, d)
            dq_buf[:, at] = flip(norm_back(dqn, unit, inv, gain).astype(BF16), d)
            return carry

        lax.fori_loop(0, grp // pair, some, 0)
        for s in range(1, blocks):
            at = slice(s * tok, (s + 1) * tok)
            grad_send[h, s - 1, :, :d] = (dk_own[at, :] * inv_root).astype(BF16)
            grad_send[h, s - 1, :, d:] = dv_own[at, :].astype(BF16)

            @pl.when(c >= s)
            def _():
                grad_copy(h, s).start()

        dk_sum[h] = dk_own[:tok, :] * inv_root
        dv_sum[h] = dv_own[:tok, :]
        out_copy(h, out_buf, out_hbm, 0).start()
        out_copy(h, dq_buf, dq_hbm, 1).start()
        return carry

    lax.fori_loop(0, kv, head, 0)

    acc_k = jnp.zeros((d, tok), F32)
    for h in range(kv):
        for s in range(1, blocks):

            @pl.when(c + s < n_cp)
            def _():
                grad_copy(h, s).wait_recv()

        dk = dk_sum[h]
        dv = dv_sum[h]
        for s in range(1, blocks):
            dk = dk + grad_recv[h, s - 1, :, :d].astype(F32)
            dv = dv + grad_recv[h, s - 1, :, d:].astype(F32)
        at = slice(h * d, (h + 1) * d)
        dv_ref[:, at] = dv.astype(BF16)
        dkn = unrotate(dk.T, cos_ref[...], sin_ref[...])
        acc_k = acc_k + dkn * k_unit[h]
        dk_ref[:, at] = norm_back(dkn, k_unit[h], k_inv[h, 0:1, :], gk_t[...]).T.astype(BF16)

    part[...] = jnp.concatenate(
        [
            jnp.sum(acc_q[...].T, axis=0, keepdims=True),
            jnp.sum(acc_k.T, axis=0, keepdims=True),
            jnp.zeros((6, d), F32),
        ],
        axis=0,
    )
    dp_recv[a] = part[...]

    def dp_copy(r):
        return pltpu.make_async_remote_copy(
            src_ref=part,
            dst_ref=dp_recv.at[a],
            send_sem=ds_sem.at[r - 1],
            recv_sem=dr_sem.at[r - 1],
            device_id={"dp": lax.rem(a + r, n_dp)},
            device_id_type=MESH,
        )

    def cp_copy(r):
        return pltpu.make_async_remote_copy(
            src_ref=tot,
            dst_ref=cp_recv.at[c],
            send_sem=cs_sem.at[r - 1],
            recv_sem=cr_sem.at[r - 1],
            device_id={"cp": lax.rem(c + r, n_cp)},
            device_id_type=MESH,
        )

    for r in range(1, n_dp):
        dp_copy(r).start()
    for r in range(1, n_dp):
        dp_copy(r).wait_recv()
    total = dp_recv[0]
    for r in range(1, n_dp):
        total = total + dp_recv[r]
    tot[...] = total
    cp_recv[c] = total

    def each(act):
        def step(r, carry):
            act(cp_copy(r))
            return carry

        lax.fori_loop(1, n_cp, step, 0)

    each(lambda copy: copy.start())

    for r in range(1, n_dp):
        kv_copy(r).wait_send()
        dp_copy(r).wait_send()
    for s in range(1, blocks):

        @pl.when(c + s < n_cp)
        def _():
            id_copy(s).wait_send()

    def settle(h, carry):
        for r in range(1, n_dp):
            qg_copy(h, r).wait_send()
        for s in range(1, blocks):

            @pl.when(c + s < n_cp)
            def _():
                ring_copy(h, s).wait_send()

            @pl.when(c >= s)
            def _():
                grad_copy(h, s).wait_send()

        out_copy(h, out_buf, out_hbm, 0).wait()
        out_copy(h, dq_buf, dq_hbm, 1).wait()
        return carry

    lax.fori_loop(0, kv, settle, 0)
    each(lambda copy: copy.wait())
    total = lax.fori_loop(1, n_cp, lambda r, sofar: sofar + cp_recv[r], cp_recv[0])
    total = total * (1.0 / math.sqrt(tok * n_dp * n_cp))
    gains_q_ref[...] = total[0:1, :]
    gains_k_ref[...] = total[1:2, :]


def body(n_dp, n_cp, q_raw, k_raw, values, loss_grad, send_order, doc_blocks, gain_q, gain_k):
    tok, q_width = q_raw.shape
    kw = k_raw.shape[1]
    d = gain_q.shape[0]
    kv = kw // d
    grp = q_width // kw
    blocks = min(MOST_BLK, n_cp)
    reach = blocks - 1
    pair = 2 if grp % 2 == 0 else 1
    assert doc_blocks.shape == (1, 1)
    frequency = THETA ** (-(np.arange(d // 2, dtype=np.float64) * 2.0 / d))
    angles = frequency[:, None] * np.arange(MOST_BLK * tok, dtype=np.float64)[None, :]
    table = jnp.asarray(np.concatenate([np.cos(angles), np.sin(angles)]).astype(np.float32))
    vmem = pl.BlockSpec(memory_space=pltpu.VMEM)
    hbm = pl.BlockSpec(memory_space=pl.ANY)
    dma = pltpu.SemaphoreType.DMA
    V = pltpu.VMEM
    outs = pl.pallas_call(
        functools.partial(kernel, n_dp, n_cp, kv, grp, d, tok, pair),
        out_shape=[
            jax.ShapeDtypeStruct((tok, q_width), BF16),
            jax.ShapeDtypeStruct((tok, q_width), BF16),
            jax.ShapeDtypeStruct((tok, kw), BF16),
            jax.ShapeDtypeStruct((tok, kw), BF16),
            jax.ShapeDtypeStruct((1, d), F32),
            jax.ShapeDtypeStruct((1, d), F32),
        ],
        in_specs=[hbm] * 4 + [vmem] * 5,
        out_specs=[hbm] * 2 + [vmem] * 4,
        scratch_shapes=[
            V((tok, q_width), BF16),
            V((tok, kw), BF16),
            V((tok, kw), BF16),
            V((tok, q_width), BF16),
            V((tok, tok), BF16),
            V((tok, 2 * kw), BF16),
            V((tok, 2 * kw), BF16),
            V((kv, tok, 2 * grp * d), BF16),
            V((kv, tok, 2 * grp * d), BF16),
            V((8, 128), jnp.int32),
            V((reach, 8, 128), jnp.int32),
            V((kv, tok, 2 * d), BF16),
            V((kv, reach, tok, 2 * d), BF16),
            V((blocks * tok, d), BF16),
            V((blocks * tok, d), BF16),
            V((d, blocks * tok), BF16),
            V((d, blocks * tok), BF16),
            V((kv, reach, tok, 2 * d), BF16),
            V((kv, reach, tok, 2 * d), BF16),
            V((blocks * tok, d), F32),
            V((blocks * tok, d), F32),
            V((kv, tok, d), F32),
            V((kv, tok, d), F32),
            V((kv, d, tok), F32),
            V((kv, 8, tok), F32),
            V((d // 2, tok), F32),
            V((d // 2, tok), F32),
            V((d, d), F32),
            V((d, d), F32),
            V((tok, tok), F32),
            V((tok, q_width), BF16),
            V((tok, q_width), BF16),
            V((d, tok), F32),
            V((8, d), F32),
            V((8, d), F32),
            V((n_dp, 8, d), F32),
            V((n_cp, 8, d), F32),
            dma((4, kv)),
            dma((2, kv)),
            dma((n_dp - 1,)),
            dma((n_dp - 1,)),
            dma((kv, n_dp - 1)),
            dma((kv, n_dp - 1)),
            dma((reach,)),
            dma((reach,)),
            dma((kv, reach)),
            dma((kv, reach)),
            dma((kv, reach)),
            dma((kv, reach)),
            dma((n_dp - 1,)),
            dma((n_dp - 1,)),
            dma((n_cp - 1,)),
            dma((n_cp - 1,)),
        ],
        compiler_params=pltpu.CompilerParams(
            collective_id=0, has_side_effects=True, vmem_limit_bytes=44 * 1024 * 1024
        ),
    )(
        q_raw, k_raw, values, loss_grad, send_order, doc_blocks,
        gain_q.reshape(1, d), gain_k.reshape(1, d), table,
    )
    return (*outs[:4], outs[4].reshape(d), outs[5].reshape(d))


def solution(mesh):
    split = P(("dp", "cp"), None)
    return jax.shard_map(
        functools.partial(body, mesh.shape["dp"], mesh.shape["cp"]),
        mesh=mesh,
        in_specs=(split,) * 5 + (P("dp", "cp"), P(), P()),
        out_specs=(split,) * 4 + (P(), P()),
        check_vma=False,
    )
```

```python
import functools
import math

import jax
import jax.numpy as jnp
import numpy as np
from jax import lax
from jax.experimental import pallas as pl
from jax.experimental.pallas import tpu as pltpu
from jax.sharding import PartitionSpec as P

MOST_BLK = 5
EPSILON = 1e-06
THETA = 1000000.0
NEGATIVE = -1e30
MESH = pl.DeviceIdType.MESH
F32 = jnp.float32
BF16 = jnp.bfloat16


def dot(a, b):
    return jnp.dot(a, b, preferred_element_type=F32)


def dot_nt(a, b):
    return lax.dot_general(a, b, (((1,), (1,)), ((), ())), preferred_element_type=F32)


def flip(x, d):
    parts = [x[:, i : i + d].T for i in range(0, x.shape[1], d)]
    return parts[0] if len(parts) == 1 else jnp.concatenate(parts, axis=1)


def wide(x, n):
    return x if n == 1 else jnp.concatenate([x] * n, axis=1)


def rotate(x, cos, sin):
    half = x.shape[0] // 2
    lead, trail = x[:half], x[half:]
    return jnp.concatenate([lead * cos - trail * sin, trail * cos + lead * sin], axis=0)


def unrotate(x, cos, sin):
    half = x.shape[0] // 2
    lead, trail = x[:half], x[half:]
    return jnp.concatenate([lead * cos + trail * sin, trail * cos - lead * sin], axis=0)


def unit_of(x):
    inv = lax.rsqrt(jnp.mean(x * x, axis=0, keepdims=True) + EPSILON)
    return x * inv, inv


def norm_back(cot, unit, inv, gain):
    scaled = cot * gain
    inner = jnp.mean(scaled * unit, axis=0, keepdims=True)
    return inv * (scaled - unit * inner)


def kernel(
    n_dp, n_cp, kv, grp, d, tok, pair,
    q_hbm, k_hbm, v_hbm, g_hbm, order_hbm, doc_ref, gq_hbm, gk_hbm, table_hbm,
    out_hbm, dq_hbm, dk_ref, dv_ref, gains_ref,
    q_in, k_in, v_in, g_in, order_ref, gq_ref, gk_ref, table_ref, hot, kv_send, kv_recv, qg_send, qg_recv,
    id_send, id_recv, ring_send, ring_recv, keys, vals, keys_t, vals_t,
    grad_send, grad_recv, dk_own, dv_own, dk_sum, dv_sum, k_unit, k_inv,
    cos_ref, sin_ref, gq_t, gk_t, tri, out_buf, dq_buf, acc_q, part, tot, dp_recv, cp_recv,
    small_sem, in_sem, out_sem, kvs_sem, kvr_sem, qgs_sem, qgr_sem, ids_sem, idr_sem,
    rs_sem, rr_sem, gs_sem, gr_sem, ds_sem, dr_sem, cs_sem, cr_sem,
):
    a = lax.axis_index("dp")
    c = lax.axis_index("cp")
    reach = min(MOST_BLK - 1, n_cp - 1)
    blocks = reach + 1
    ahead = 2
    width = grp * d
    rows = tok // n_dp
    inv_root = 1.0 / math.sqrt(d)
    exp_scale = inv_root * math.log2(math.e)

    def columns(h, size):
        return pl.ds(pl.multiple_of(h * size, size), size)

    def in_copy(h, src, dst, which):
        return pltpu.make_async_copy(
            src.at[:, columns(h, width)], dst.at[:, columns(h, width)], in_sem.at[2 + which, h]
        )

    k_copy = pltpu.make_async_copy(k_hbm, k_in, in_sem.at[0, 0])
    v_copy = pltpu.make_async_copy(v_hbm, v_in, in_sem.at[1, 0])
    small = [
        pltpu.make_async_copy(src, dst, small_sem.at[i])
        for i, (src, dst) in enumerate(
            [(order_hbm, order_ref), (gq_hbm, gq_ref), (gk_hbm, gk_ref), (table_hbm, table_ref)]
        )
    ]
    small[0].start()
    k_copy.start()
    v_copy.start()
    for copy in small[1:]:
        copy.start()
    for h in range(kv):
        in_copy(h, q_hbm, q_in, 0).start()
        in_copy(h, g_hbm, g_in, 1).start()

    barrier = pltpu.get_barrier_semaphore()
    for r in range(1, n_dp):
        pl.semaphore_signal(
            barrier, inc=1, device_id={"dp": lax.rem(a + r, n_dp)}, device_id_type=MESH
        )

    def greet(r, carry):
        pl.semaphore_signal(
            barrier, inc=1, device_id={"cp": lax.rem(c + r, n_cp)}, device_id_type=MESH
        )
        return carry

    lax.fori_loop(1, n_cp, greet, 0)

    own_id = jnp.broadcast_to(doc_ref[...], (8, 128))
    id_send[...] = own_id
    small[0].wait()
    order = jnp.broadcast_to(order_ref[...], (tok, tok)).astype(F32).T
    slot = lax.broadcasted_iota(jnp.int32, (tok, tok), 1)
    hot[...] = jnp.where(order == slot.astype(F32), 1.0, 0.0).astype(BF16)
    small[1].wait()
    small[2].wait()
    gq_t[...] = jnp.broadcast_to(gq_ref[...], (d, d)).T
    gk_t[...] = jnp.broadcast_to(gk_ref[...], (d, d)).T
    tri[...] = jnp.where(
        lax.broadcasted_iota(jnp.int32, (tok, tok), 0)
        <= lax.broadcasted_iota(jnp.int32, (tok, tok), 1),
        0.0,
        NEGATIVE,
    )
    acc_q[...] = jnp.zeros_like(acc_q)
    for s in range(1, blocks):

        @pl.when(c < s)
        def _():
            id_recv[s - 1] = jnp.zeros((8, 128), jnp.int32)
            for h in range(kv):
                ring_recv[h, s - 1] = jnp.zeros((tok, 2 * d), BF16)

        @pl.when(c + s >= n_cp)
        def _():
            for h in range(kv):
                grad_recv[h, s - 1] = jnp.zeros((tok, 2 * d), BF16)

    k_copy.wait()
    v_copy.wait()
    kw = kv * d
    kv_send[:, :kw] = dot(hot[...], k_in[...]).astype(BF16)
    kv_send[:, kw:] = dot(hot[...], v_in[...]).astype(BF16)
    mine = pl.ds(pl.multiple_of(a * rows, rows), rows)
    kv_recv[mine, :] = kv_send[mine, :]

    pl.semaphore_wait(barrier, n_dp - 1 + n_cp - 1)

    def kv_copy(r):
        peer = lax.rem(a + r, n_dp)
        return pltpu.make_async_remote_copy(
            src_ref=kv_send.at[pl.ds(pl.multiple_of(peer * rows, rows), rows), :],
            dst_ref=kv_recv.at[mine, :],
            send_sem=kvs_sem.at[r - 1],
            recv_sem=kvr_sem.at[r - 1],
            device_id={"dp": peer},
            device_id_type=MESH,
        )

    def qg_copy(h, r):
        peer = lax.rem(a + r, n_dp)
        return pltpu.make_async_remote_copy(
            src_ref=qg_send.at[h, pl.ds(pl.multiple_of(peer * rows, rows), rows), :],
            dst_ref=qg_recv.at[h, mine, :],
            send_sem=qgs_sem.at[h, r - 1],
            recv_sem=qgr_sem.at[h, r - 1],
            device_id={"dp": peer},
            device_id_type=MESH,
        )

    def id_copy(s):
        return pltpu.make_async_remote_copy(
            src_ref=id_send,
            dst_ref=id_recv.at[s - 1],
            send_sem=ids_sem.at[s - 1],
            recv_sem=idr_sem.at[s - 1],
            device_id={"cp": lax.rem(c + s, n_cp)},
            device_id_type=MESH,
        )

    def ring_copy(h, s):
        return pltpu.make_async_remote_copy(
            src_ref=ring_send.at[h],
            dst_ref=ring_recv.at[h, s - 1],
            send_sem=rs_sem.at[h, s - 1],
            recv_sem=rr_sem.at[h, s - 1],
            device_id={"cp": lax.rem(c + s, n_cp)},
            device_id_type=MESH,
        )

    def grad_copy(h, s):
        return pltpu.make_async_remote_copy(
            src_ref=grad_send.at[h, s - 1],
            dst_ref=grad_recv.at[h, s - 1],
            send_sem=gs_sem.at[h, s - 1],
            recv_sem=gr_sem.at[h, s - 1],
            device_id={"cp": lax.rem(c + n_cp - s, n_cp)},
            device_id_type=MESH,
        )

    for r in range(1, n_dp):
        kv_copy(r).start()
    for s in range(1, blocks):

        @pl.when(c + s < n_cp)
        def _():
            id_copy(s).start()

    def gather(h, carry):
        in_copy(h, q_hbm, q_in, 0).wait()
        in_copy(h, g_hbm, g_in, 1).wait()
        qg_send[h, :, :width] = dot(hot[...], q_in[:, columns(h, width)]).astype(BF16)
        qg_send[h, :, width:] = dot(hot[...], g_in[:, columns(h, width)]).astype(BF16)
        qg_recv[h, mine, :] = qg_send[h, mine, :]

        @pl.when(h < ahead)
        def _():
            for r in range(1, n_dp):
                qg_copy(h, r).start()

        return carry

    lax.fori_loop(0, kv, gather, 0)

    for s in range(1, blocks):

        @pl.when(c >= s)
        def _():
            id_copy(s).wait_recv()

    before = jnp.zeros((1, 128), F32)
    away = []
    for s in range(1, blocks):
        here = (c >= s).astype(F32)
        same = jnp.where(id_recv[s - 1, 0:1, :] == own_id[0:1, :], here, 0.0)
        before = before + same
        away.append(wide((1.0 - same) * -NEGATIVE, pair))
    small[3].wait()
    half = d // 2
    cos = jnp.zeros((half, tok), F32)
    sin = jnp.zeros((half, tok), F32)
    for s in range(MOST_BLK):
        hit = before == float(s)
        cos = cos + jnp.where(hit, table_ref[:half, s * tok : (s + 1) * tok], 0.0)
        sin = sin + jnp.where(hit, table_ref[half:, s * tok : (s + 1) * tok], 0.0)
    cos_ref[...] = cos
    sin_ref[...] = sin

    for r in range(1, n_dp):
        kv_copy(r).wait_recv()

    for h in range(kv):
        x = kv_recv[:, h * d : (h + 1) * d].astype(F32).T
        unit, inv = unit_of(x)
        k_unit[h] = unit
        k_inv[h] = jnp.broadcast_to(inv, (8, tok))
        turned = rotate(unit * gk_t[...], cos_ref[...], sin_ref[...])
        ring_send[h, :, :d] = turned.T.astype(BF16)
        ring_send[h, :, d:] = kv_recv[:, kw + h * d : kw + (h + 1) * d]
        for s in range(1, blocks):

            @pl.when((c + s < n_cp) & (h < ahead))
            def _():
                ring_copy(h, s).start()

    def out_copy(h, src, dst, which):
        return pltpu.make_async_copy(
            src.at[:, columns(h, width)], dst.at[:, columns(h, width)], out_sem.at[which, h]
        )

    span = pair * d

    def head(h, carry):
        for r in range(1, n_dp):
            qg_copy(h, r).wait_recv()
        for s in range(1, blocks):

            @pl.when(c >= s)
            def _():
                ring_copy(h, s).wait_recv()

        @pl.when(h + ahead < kv)
        def _():
            for r in range(1, n_dp):
                qg_copy(h + ahead, r).start()
        for s in range(1, blocks):

            @pl.when((c + s < n_cp) & (h + ahead < kv))
            def _():
                ring_copy(h + ahead, s).start()

        for s in range(blocks):
            both = ring_send[h] if s == 0 else ring_recv[h, s - 1]
            keys[s * tok : (s + 1) * tok, :] = both[:, :d]
            vals[s * tok : (s + 1) * tok, :] = both[:, d:]
            keys_t[:, s * tok : (s + 1) * tok] = both[:, :d].T
            vals_t[:, s * tok : (s + 1) * tok] = both[:, d:].T
        dk_own[...] = jnp.zeros_like(dk_own)
        dv_own[...] = jnp.zeros_like(dv_own)

        def some(j, carry):
            cos = wide(cos_ref[...], pair)
            sin = wide(sin_ref[...], pair)
            gain = wide(gq_t[...], pair)
            unit, inv = unit_of(flip(qg_recv[h, :, columns(j, span)], d).astype(F32))
            turned = rotate(unit * gain, cos, sin).astype(BF16)
            g_at = pl.ds(pl.multiple_of(width + j * span, span), span)
            g_rows = qg_recv[h, :, g_at]
            g_t = flip(g_rows, d)
            g_rows = jnp.concatenate(
                [g_rows[:, i * d : (i + 1) * d] for i in range(pair)], axis=0
            )
            scores = dot(keys[...], turned)
            parts = [scores[s * tok : (s + 1) * tok] for s in range(blocks)]
            parts[0] = parts[0] + wide(tri[...], pair)
            top = jnp.max(parts[0], axis=0, keepdims=True)
            for s in range(1, blocks):
                top = jnp.maximum(top, jnp.max(parts[s], axis=0, keepdims=True) - away[s - 1])
            weights = [
                jnp.exp2((parts[s] - (top if s == 0 else top + away[s - 1])) * exp_scale)
                for s in range(blocks)
            ]
            weights = jnp.concatenate(weights, axis=0)
            inv_sum = 1.0 / jnp.sum(weights, axis=0, keepdims=True)
            out_t = (dot(vals_t[...], weights.astype(BF16)) * inv_sum).astype(BF16)
            delta = jnp.sum(g_t.astype(F32) * out_t.astype(F32), axis=0, keepdims=True)
            probs = weights * inv_sum
            dprobs = dot(vals[...], g_t)
            dscores = (probs * (dprobs - delta)).astype(BF16)
            dk_own[...] += dot_nt(dscores, turned)
            dv_own[...] += dot(probs.astype(BF16), g_rows)
            dqn = unrotate(dot(keys_t[...], dscores) * inv_root, cos, sin)
            term = dqn * unit
            acc_q[...] += sum(term[:, i * d : (i + 1) * d] for i in range(pair))
            at = pl.ds(pl.multiple_of(h * width + j * span, span), span)
            out_buf[:, at] = flip(out_t, d)
            dq_buf[:, at] = flip(norm_back(dqn, unit, inv, gain).astype(BF16), d)
            return carry

        lax.fori_loop(0, grp // pair, some, 0)
        for s in range(1, blocks):
            at = slice(s * tok, (s + 1) * tok)
            grad_send[h, s - 1, :, :d] = (dk_own[at, :] * inv_root).astype(BF16)
            grad_send[h, s - 1, :, d:] = dv_own[at, :].astype(BF16)

            @pl.when(c >= s)
            def _():
                grad_copy(h, s).start()

        dk_sum[h] = dk_own[:tok, :] * inv_root
        dv_sum[h] = dv_own[:tok, :]
        out_copy(h, out_buf, out_hbm, 0).start()
        out_copy(h, dq_buf, dq_hbm, 1).start()
        return carry

    lax.fori_loop(0, kv, head, 0)

    acc_k = jnp.zeros((d, tok), F32)
    for h in range(kv):
        for s in range(1, blocks):

            @pl.when(c + s < n_cp)
            def _():
                grad_copy(h, s).wait_recv()

        dk = dk_sum[h]
        dv = dv_sum[h]
        for s in range(1, blocks):
            dk = dk + grad_recv[h, s - 1, :, :d].astype(F32)
            dv = dv + grad_recv[h, s - 1, :, d:].astype(F32)
        at = slice(h * d, (h + 1) * d)
        dv_ref[:, at] = dv.astype(BF16)
        dkn = unrotate(dk.T, cos_ref[...], sin_ref[...])
        acc_k = acc_k + dkn * k_unit[h]
        dk_ref[:, at] = norm_back(dkn, k_unit[h], k_inv[h, 0:1, :], gk_t[...]).T.astype(BF16)

    part[...] = jnp.concatenate(
        [
            jnp.sum(acc_q[...].T, axis=0, keepdims=True),
            jnp.sum(acc_k.T, axis=0, keepdims=True),
            jnp.zeros((6, d), F32),
        ],
        axis=0,
    )
    dp_recv[a] = part[...]

    def dp_copy(r):
        return pltpu.make_async_remote_copy(
            src_ref=part,
            dst_ref=dp_recv.at[a],
            send_sem=ds_sem.at[r - 1],
            recv_sem=dr_sem.at[r - 1],
            device_id={"dp": lax.rem(a + r, n_dp)},
            device_id_type=MESH,
        )

    def cp_copy(r):
        return pltpu.make_async_remote_copy(
            src_ref=tot,
            dst_ref=cp_recv.at[c],
            send_sem=cs_sem.at[r - 1],
            recv_sem=cr_sem.at[r - 1],
            device_id={"cp": lax.rem(c + r, n_cp)},
            device_id_type=MESH,
        )

    for r in range(1, n_dp):
        dp_copy(r).start()
    for r in range(1, n_dp):
        dp_copy(r).wait_recv()
    total = dp_recv[0]
    for r in range(1, n_dp):
        total = total + dp_recv[r]
    tot[...] = total
    cp_recv[c] = total

    def each(act):
        def step(r, carry):
            act(cp_copy(r))
            return carry

        lax.fori_loop(1, n_cp, step, 0)

    each(lambda copy: copy.start())

    for r in range(1, n_dp):
        kv_copy(r).wait_send()
        dp_copy(r).wait_send()
    for s in range(1, blocks):

        @pl.when(c + s < n_cp)
        def _():
            id_copy(s).wait_send()

    def settle(h, carry):
        for r in range(1, n_dp):
            qg_copy(h, r).wait_send()
        for s in range(1, blocks):

            @pl.when(c + s < n_cp)
            def _():
                ring_copy(h, s).wait_send()

            @pl.when(c >= s)
            def _():
                grad_copy(h, s).wait_send()

        out_copy(h, out_buf, out_hbm, 0).wait()
        out_copy(h, dq_buf, dq_hbm, 1).wait()
        return carry

    lax.fori_loop(0, kv, settle, 0)
    each(lambda copy: copy.wait())
    total = lax.fori_loop(1, n_cp, lambda r, sofar: sofar + cp_recv[r], cp_recv[0])
    total = total * (1.0 / math.sqrt(tok * n_dp * n_cp))
    gains_ref[...] = total


def hand_out(out, dq, dk, dv, gains, out_o, dq_o, dk_o, dv_o, gq_o, gk_o, sem):
    pairs = [
        (out, out_o), (dq, dq_o), (dk, dk_o), (dv, dv_o),
        (gains.at[0:1], gq_o), (gains.at[1:2], gk_o),
    ]
    copies = [pltpu.make_async_copy(src, dst, sem.at[i]) for i, (src, dst) in enumerate(pairs)]
    for copy in copies:
        copy.start()
    for copy in copies:
        copy.wait()


def body(n_dp, n_cp, q_raw, k_raw, values, loss_grad, send_order, doc_blocks, gain_q, gain_k):
    tok, q_width = q_raw.shape
    kw = k_raw.shape[1]
    d = gain_q.shape[0]
    kv = kw // d
    grp = q_width // kw
    blocks = min(MOST_BLK, n_cp)
    reach = blocks - 1
    pair = 4 if grp % 4 == 0 else 1
    assert doc_blocks.shape == (1, 1)
    frequency = THETA ** (-(np.arange(d // 2, dtype=np.float64) * 2.0 / d))
    angles = frequency[:, None] * np.arange(MOST_BLK * tok, dtype=np.float64)[None, :]
    table = jnp.asarray(np.concatenate([np.cos(angles), np.sin(angles)]).astype(np.float32))
    vmem = pl.BlockSpec(memory_space=pltpu.VMEM)
    hbm = pl.BlockSpec(memory_space=pltpu.HBM)
    anywhere = pl.BlockSpec(memory_space=pl.ANY)
    dma = pltpu.SemaphoreType.DMA
    V = pltpu.VMEM
    outs = pl.pallas_call(
        functools.partial(kernel, n_dp, n_cp, kv, grp, d, tok, pair),
        out_shape=[
            jax.ShapeDtypeStruct((tok, q_width), BF16),
            jax.ShapeDtypeStruct((tok, q_width), BF16),
            jax.ShapeDtypeStruct((tok, kw), BF16),
            jax.ShapeDtypeStruct((tok, kw), BF16),
            jax.ShapeDtypeStruct((8, d), F32),
        ],
        in_specs=[hbm] * 5 + [vmem] + [hbm] * 3,
        out_specs=[anywhere] * 2 + [vmem] * 3,
        scratch_shapes=[
            V((tok, q_width), BF16),
            V((tok, kw), BF16),
            V((tok, kw), BF16),
            V((tok, q_width), BF16),
            V((1, tok), jnp.int32),
            V((1, d), F32),
            V((1, d), F32),
            V(table.shape, F32),
            V((tok, tok), BF16),
            V((tok, 2 * kw), BF16),
            V((tok, 2 * kw), BF16),
            V((kv, tok, 2 * grp * d), BF16),
            V((kv, tok, 2 * grp * d), BF16),
            V((8, 128), jnp.int32),
            V((reach, 8, 128), jnp.int32),
            V((kv, tok, 2 * d), BF16),
            V((kv, reach, tok, 2 * d), BF16),
            V((blocks * tok, d), BF16),
            V((blocks * tok, d), BF16),
            V((d, blocks * tok), BF16),
            V((d, blocks * tok), BF16),
            V((kv, reach, tok, 2 * d), BF16),
            V((kv, reach, tok, 2 * d), BF16),
            V((blocks * tok, d), F32),
            V((blocks * tok, d), F32),
            V((kv, tok, d), F32),
            V((kv, tok, d), F32),
            V((kv, d, tok), F32),
            V((kv, 8, tok), F32),
            V((d // 2, tok), F32),
            V((d // 2, tok), F32),
            V((d, d), F32),
            V((d, d), F32),
            V((tok, tok), F32),
            V((tok, q_width), BF16),
            V((tok, q_width), BF16),
            V((d, tok), F32),
            V((8, d), F32),
            V((8, d), F32),
            V((n_dp, 8, d), F32),
            V((n_cp, 8, d), F32),
            dma((4,)),
            dma((4, kv)),
            dma((2, kv)),
            dma((n_dp - 1,)),
            dma((n_dp - 1,)),
            dma((kv, n_dp - 1)),
            dma((kv, n_dp - 1)),
            dma((reach,)),
            dma((reach,)),
            dma((kv, reach)),
            dma((kv, reach)),
            dma((kv, reach)),
            dma((kv, reach)),
            dma((n_dp - 1,)),
            dma((n_dp - 1,)),
            dma((n_cp - 1,)),
            dma((n_cp - 1,)),
        ],
        compiler_params=pltpu.CompilerParams(
            collective_id=0, has_side_effects=True, vmem_limit_bytes=60 * 1024 * 1024
        ),
    )(
        q_raw, k_raw, values, loss_grad, send_order, doc_blocks,
        gain_q.reshape(1, d), gain_k.reshape(1, d), table,
    )
    outs = pl.pallas_call(
        hand_out,
        out_shape=[jax.ShapeDtypeStruct(x.shape, x.dtype) for x in outs[:4]]
        + [jax.ShapeDtypeStruct((1, d), F32)] * 2,
        in_specs=[anywhere] * 4 + [vmem],
        out_specs=[hbm] * 6,
        scratch_shapes=[dma((6,))],
        compiler_params=pltpu.CompilerParams(vmem_limit_bytes=60 * 1024 * 1024),
    )(*outs)
    return (*outs[:4], outs[4].reshape(d), outs[5].reshape(d))


def solution(mesh):
    split = P(("dp", "cp"), None)
    return jax.shard_map(
        functools.partial(body, mesh.shape["dp"], mesh.shape["cp"]),
        mesh=mesh,
        in_specs=(split,) * 5 + (P("dp", "cp"), P(), P()),
        out_specs=(split,) * 4 + (P(), P()),
        check_vma=False,
    )
```

```python
import functools
import math

import jax
import jax.numpy as jnp
import numpy as np
from jax import lax
from jax.experimental import pallas as pl
from jax.experimental.pallas import tpu as pltpu
from jax.sharding import PartitionSpec as P

MOST_BLK = 5
EPSILON = 1e-06
THETA = 1000000.0
NEGATIVE = -1e30
MESH = pl.DeviceIdType.MESH
F32 = jnp.float32
BF16 = jnp.bfloat16


def dot(a, b):
    return jnp.dot(a, b, preferred_element_type=F32)


def dot_nt(a, b):
    return lax.dot_general(a, b, (((1,), (1,)), ((), ())), preferred_element_type=F32)


def flip(x, d):
    parts = [x[:, i : i + d].T for i in range(0, x.shape[1], d)]
    return parts[0] if len(parts) == 1 else jnp.concatenate(parts, axis=1)


def wide(x, n):
    return x if n == 1 else jnp.concatenate([x] * n, axis=1)


def rotate(x, cos, sin):
    half = x.shape[0] // 2
    lead, trail = x[:half], x[half:]
    return jnp.concatenate([lead * cos - trail * sin, trail * cos + lead * sin], axis=0)


def unrotate(x, cos, sin):
    half = x.shape[0] // 2
    lead, trail = x[:half], x[half:]
    return jnp.concatenate([lead * cos + trail * sin, trail * cos - lead * sin], axis=0)


def unit_of(x):
    inv = lax.rsqrt(jnp.mean(x * x, axis=0, keepdims=True) + EPSILON)
    return x * inv, inv


def norm_back(cot, unit, inv, gain):
    scaled = cot * gain
    inner = jnp.mean(scaled * unit, axis=0, keepdims=True)
    return inv * (scaled - unit * inner)


def kernel(
    n_dp, n_cp, kv, grp, d, tok, pair,
    q_hbm, k_hbm, v_hbm, g_hbm, order_hbm, doc_ref, gq_hbm, gk_hbm, table_hbm,
    out_hbm, dq_hbm, dk_ref, dv_ref, gains_ref,
    q_in, k_in, v_in, g_in, order_ref, gq_ref, gk_ref, table_ref, hot, kv_send, kv_recv, qg_send, qg_recv,
    id_send, id_recv, ring_send, ring_recv, keys, vals, keys_t, vals_t,
    grad_send, gy_recv, gz_recv, dk_own, dv_own, sums, k_unit, k_inv,
    cos_ref, sin_ref, gq_t, gk_t, tri, out_buf, dq_buf, acc_q, part, tot, dp_recv, cp_recv,
    small_sem, in_sem, out_sem, kvs_sem, kvr_sem, qgs_sem, qgr_sem, ids_sem, idr_sem,
    rs_sem, rr_sem, gys_sem, gyr_sem, gzs_sem, gzr_sem, ds_sem, dr_sem, cs_sem, cr_sem,
):
    a = lax.axis_index("dp")
    c = lax.axis_index("cp")
    reach = min(MOST_BLK - 1, n_cp - 1)
    blocks = reach + 1
    ahead = min(3, kv)
    even = lax.rem(c, 2) == 0
    even_f = even.astype(F32)
    mate = c + 1 - 2 * lax.rem(c, 2)
    width = grp * d
    rows = tok // n_dp
    inv_root = 1.0 / math.sqrt(d)

    def columns(h, size):
        return pl.ds(pl.multiple_of(h * size, size), size)

    def in_copy(h, src, dst, which):
        return pltpu.make_async_copy(
            src.at[:, columns(h, width)], dst.at[:, columns(h, width)], in_sem.at[2 + which, h]
        )

    k_copy = pltpu.make_async_copy(k_hbm, k_in, in_sem.at[0, 0])
    v_copy = pltpu.make_async_copy(v_hbm, v_in, in_sem.at[1, 0])
    small = [
        pltpu.make_async_copy(src, dst, small_sem.at[i])
        for i, (src, dst) in enumerate(
            [(order_hbm, order_ref), (gq_hbm, gq_ref), (gk_hbm, gk_ref), (table_hbm, table_ref)]
        )
    ]
    small[0].start()
    k_copy.start()
    v_copy.start()
    for copy in small[1:]:
        copy.start()
    for h in range(kv):
        in_copy(h, q_hbm, q_in, 0).start()
        in_copy(h, g_hbm, g_in, 1).start()

    barrier = pltpu.get_barrier_semaphore()
    for r in range(1, n_dp):
        pl.semaphore_signal(
            barrier, inc=1, device_id={"dp": lax.rem(a + r, n_dp)}, device_id_type=MESH
        )

    def greet(r, carry):
        pl.semaphore_signal(
            barrier, inc=1, device_id={"cp": lax.rem(c + r, n_cp)}, device_id_type=MESH
        )
        return carry

    lax.fori_loop(1, n_cp, greet, 0)

    own_id = jnp.broadcast_to(doc_ref[...], (8, 128))
    id_send[...] = own_id
    small[0].wait()
    order = jnp.broadcast_to(order_ref[...], (tok, tok)).astype(F32).T
    slot = lax.broadcasted_iota(jnp.int32, (tok, tok), 1)
    hot[...] = jnp.where(order == slot.astype(F32), 1.0, 0.0).astype(BF16)
    small[1].wait()
    small[2].wait()
    gq_t[...] = jnp.broadcast_to(gq_ref[...], (d, d)).T
    gk_t[...] = jnp.broadcast_to(gk_ref[...], (d, d)).T
    tri[...] = jnp.where(
        lax.broadcasted_iota(jnp.int32, (tok, tok), 0)
        <= lax.broadcasted_iota(jnp.int32, (tok, tok), 1),
        0.0,
        NEGATIVE,
    )
    acc_q[...] = jnp.zeros_like(acc_q)
    for s in range(1, blocks):

        @pl.when(c < s)
        def _():
            id_recv[s - 1] = jnp.zeros((8, 128), jnp.int32)
            for h in range(kv):
                ring_recv[h, s - 1] = jnp.zeros((tok, 2 * d), BF16)

    blank = jnp.zeros((tok, 2 * d), BF16)
    for slot_of, missing in (
        ((0, 0), mate < 1),
        ((0, 1), mate < 3),
        ((1, 0), (c + 2 >= n_cp) | (c < 2)),
        ((1, 1), c + 2 >= n_cp),
    ):

        @pl.when(missing)
        def _():
            for h in range(kv):
                (gy_recv if slot_of[0] == 0 else gz_recv)[h, slot_of[1]] = blank

    k_copy.wait()
    v_copy.wait()
    kw = kv * d
    kv_send[:, :kw] = dot(hot[...], k_in[...]).astype(BF16)
    kv_send[:, kw:] = dot(hot[...], v_in[...]).astype(BF16)
    mine = pl.ds(pl.multiple_of(a * rows, rows), rows)
    kv_recv[mine, :] = kv_send[mine, :]

    pl.semaphore_wait(barrier, n_dp - 1 + n_cp - 1)

    def kv_copy(r):
        peer = lax.rem(a + r, n_dp)
        return pltpu.make_async_remote_copy(
            src_ref=kv_send.at[pl.ds(pl.multiple_of(peer * rows, rows), rows), :],
            dst_ref=kv_recv.at[mine, :],
            send_sem=kvs_sem.at[r - 1],
            recv_sem=kvr_sem.at[r - 1],
            device_id={"dp": peer},
            device_id_type=MESH,
        )

    def qg_copy(h, r):
        peer = lax.rem(a + r, n_dp)
        return pltpu.make_async_remote_copy(
            src_ref=qg_send.at[h, pl.ds(pl.multiple_of(peer * rows, rows), rows), :],
            dst_ref=qg_recv.at[h, mine, :],
            send_sem=qgs_sem.at[h, r - 1],
            recv_sem=qgr_sem.at[h, r - 1],
            device_id={"dp": peer},
            device_id_type=MESH,
        )

    def id_copy(s):
        return pltpu.make_async_remote_copy(
            src_ref=id_send,
            dst_ref=id_recv.at[s - 1],
            send_sem=ids_sem.at[s - 1],
            recv_sem=idr_sem.at[s - 1],
            device_id={"cp": lax.rem(c + s, n_cp)},
            device_id_type=MESH,
        )

    def ring_copy(h, src, to, s, kind):
        return pltpu.make_async_remote_copy(
            src_ref=src,
            dst_ref=ring_recv.at[h, s - 1],
            send_sem=rs_sem.at[h, kind],
            recv_sem=rr_sem.at[h, s - 1],
            device_id={"cp": to},
            device_id_type=MESH,
        )

    behind = lax.rem(c + 2, n_cp)
    front = lax.rem(c + n_cp - 2, n_cp)

    def ring_plan(h):
        own, two, four = ring_send.at[h], ring_recv.at[h, 1], ring_recv.at[h, 3]
        return (
            (ring_copy(h, own, behind, 2, 0), c + 2 < n_cp),
            (ring_copy(h, own, mate, 1, 2), even),
            (ring_copy(h, two, behind, 4, 1), (c >= 2) & (c + 2 < n_cp)),
            (ring_copy(h, two, mate, 3, 3), even & (c >= 2)),
            (ring_copy(h, two, mate, 1, 2), jnp.logical_not(even) & (c >= 2)),
            (ring_copy(h, four, mate, 3, 3), jnp.logical_not(even) & (c >= 4)),
        )

    def ring_arrived(h, s):
        @pl.when(c >= s)
        def _():
            ring_copy(h, ring_send.at[h], mate, s, 0).wait_recv()

    def start_if(plan):
        copy, wanted = plan

        @pl.when(wanted)
        def _():
            copy.start()

    def mate_copy(h, i):
        return pltpu.make_async_remote_copy(
            src_ref=grad_send.at[h, 2 * i],
            dst_ref=gy_recv.at[h, i],
            send_sem=gys_sem.at[h, i],
            recv_sem=gyr_sem.at[h, i],
            device_id={"cp": mate},
            device_id_type=MESH,
        )

    def front_copy(h, i):
        return pltpu.make_async_remote_copy(
            src_ref=grad_send.at[h, 3 - 2 * i],
            dst_ref=gz_recv.at[h, i],
            send_sem=gzs_sem.at[h, i],
            recv_sem=gzr_sem.at[h, i],
            device_id={"cp": front},
            device_id_type=MESH,
        )

    def after_mate(h):
        for i in range(2):

            @pl.when(mate >= 1 + 2 * i)
            def _():
                mate_copy(h, i).wait_recv()

        one = gy_recv[h, 0].astype(F32)
        three = gy_recv[h, 1].astype(F32)
        sums[h, 0] = sums[h, 0] + one * even_f
        sums[h, 1] = sums[h, 1] + three * even_f + one * (1.0 - even_f)
        grad_send[h, 3] = (sums[h, 2] + three * (1.0 - even_f)).astype(BF16)

        @pl.when(c >= 4)
        def _():
            front_copy(h, 0).start()

    def after_four(h):
        @pl.when((c + 2 < n_cp) & (c >= 2))
        def _():
            front_copy(h, 0).wait_recv()

        grad_send[h, 1] = (sums[h, 1] + gz_recv[h, 0].astype(F32)).astype(BF16)

        @pl.when(c >= 2)
        def _():
            front_copy(h, 1).start()

    for r in range(1, n_dp):
        kv_copy(r).start()
    for s in range(1, blocks):

        @pl.when(c + s < n_cp)
        def _():
            id_copy(s).start()

    def gather(h, carry):
        in_copy(h, q_hbm, q_in, 0).wait()
        in_copy(h, g_hbm, g_in, 1).wait()
        qg_send[h, :, :width] = dot(hot[...], q_in[:, columns(h, width)]).astype(BF16)
        qg_send[h, :, width:] = dot(hot[...], g_in[:, columns(h, width)]).astype(BF16)
        qg_recv[h, mine, :] = qg_send[h, mine, :]

        @pl.when(h < ahead)
        def _():
            for r in range(1, n_dp):
                qg_copy(h, r).start()

        return carry

    lax.fori_loop(0, kv, gather, 0)

    for s in range(1, blocks):

        @pl.when(c >= s)
        def _():
            id_copy(s).wait_recv()

    before = jnp.zeros((1, 128), F32)
    away = []
    for s in range(1, blocks):
        here = (c >= s).astype(F32)
        same = jnp.where(id_recv[s - 1, 0:1, :] == own_id[0:1, :], here, 0.0)
        before = before + same
        away.append(wide((1.0 - same) * -NEGATIVE, pair))
    small[3].wait()
    half = d // 2
    cos = jnp.zeros((half, tok), F32)
    sin = jnp.zeros((half, tok), F32)
    for s in range(MOST_BLK):
        hit = before == float(s)
        cos = cos + jnp.where(hit, table_ref[:half, s * tok : (s + 1) * tok], 0.0)
        sin = sin + jnp.where(hit, table_ref[half:, s * tok : (s + 1) * tok], 0.0)
    cos_ref[...] = cos
    sin_ref[...] = sin

    for r in range(1, n_dp):
        kv_copy(r).wait_recv()

    for h in range(kv):
        x = kv_recv[:, h * d : (h + 1) * d].astype(F32).T
        unit, inv = unit_of(x)
        k_unit[h] = unit
        k_inv[h] = jnp.broadcast_to(inv, (8, tok))
        turned = rotate(unit * gk_t[...], cos_ref[...], sin_ref[...])
        ring_send[h, :, :d] = turned.T.astype(BF16)
        ring_send[h, :, d:] = kv_recv[:, kw + h * d : kw + (h + 1) * d]
        for plan in ring_plan(h)[:2]:
            start_if(plan)
    for h in range(kv):
        ring_arrived(h, 2)
        for plan in ring_plan(h)[2:5]:
            start_if(plan)
    for h in range(kv):
        ring_arrived(h, 4)
        start_if(ring_plan(h)[5])

    def out_copy(h, src, dst, which):
        return pltpu.make_async_copy(
            src.at[:, columns(h, width)], dst.at[:, columns(h, width)], out_sem.at[which, h]
        )

    span = pair * d

    def head(h, carry):
        for r in range(1, n_dp):
            qg_copy(h, r).wait_recv()
        ring_arrived(h, 1)
        ring_arrived(h, 3)

        @pl.when(h + ahead < kv)
        def _():
            for r in range(1, n_dp):
                qg_copy(h + ahead, r).start()
        for s in range(blocks):
            both = ring_send[h] if s == 0 else ring_recv[h, s - 1]
            keys[s * tok : (s + 1) * tok, :] = both[:, :d]
            vals[s * tok : (s + 1) * tok, :] = both[:, d:]
            keys_t[:, s * tok : (s + 1) * tok] = both[:, :d].T
            vals_t[:, s * tok : (s + 1) * tok] = both[:, d:].T
        dk_own[...] = jnp.zeros_like(dk_own)
        dv_own[...] = jnp.zeros_like(dv_own)

        def some(j, carry):
            cos = wide(cos_ref[...], pair)
            sin = wide(sin_ref[...], pair)
            gain = wide(gq_t[...], pair)
            unit, inv = unit_of(flip(qg_recv[h, :, columns(j, span)], d).astype(F32))
            turned = rotate(unit * gain, cos, sin).astype(BF16)
            g_at = pl.ds(pl.multiple_of(width + j * span, span), span)
            g_rows = qg_recv[h, :, g_at]
            g_t = flip(g_rows, d)
            g_rows = jnp.concatenate(
                [g_rows[:, i * d : (i + 1) * d] for i in range(pair)], axis=0
            )
            scores = dot(keys[...], turned)
            parts = [scores[s * tok : (s + 1) * tok] for s in range(blocks)]
            parts[0] = parts[0] + wide(tri[...], pair)
            top = jnp.max(parts[0], axis=0, keepdims=True)
            for s in range(1, blocks):
                top = jnp.maximum(top, jnp.max(parts[s], axis=0, keepdims=True) - away[s - 1])
            weights = [
                jnp.exp((parts[s] - (top if s == 0 else top + away[s - 1])) * inv_root)
                for s in range(blocks)
            ]
            weights = jnp.concatenate(weights, axis=0)
            inv_sum = 1.0 / jnp.sum(weights, axis=0, keepdims=True)
            out_t = (dot(vals_t[...], weights.astype(BF16)) * inv_sum).astype(BF16)
            delta = jnp.sum(g_t.astype(F32) * out_t.astype(F32), axis=0, keepdims=True)
            probs = weights * inv_sum
            dprobs = dot(vals[...], g_t)
            dscores = (probs * (dprobs - delta)).astype(BF16)
            dk_own[...] += dot_nt(dscores, turned)
            dv_own[...] += dot(probs.astype(BF16), g_rows)
            dqn = unrotate(dot(keys_t[...], dscores) * inv_root, cos, sin)
            term = dqn * unit
            acc_q[...] += sum(term[:, i * d : (i + 1) * d] for i in range(pair))
            at = pl.ds(pl.multiple_of(h * width + j * span, span), span)
            out_buf[:, at] = flip(out_t, d)
            dq_buf[:, at] = flip(norm_back(dqn, unit, inv, gain).astype(BF16), d)
            return carry

        lax.fori_loop(0, grp // pair, some, 0)
        for s in range(blocks):
            at = slice(s * tok, (s + 1) * tok)
            if s % 2 == 1:
                grad_send[h, s - 1, :, :d] = (dk_own[at, :] * inv_root).astype(BF16)
                grad_send[h, s - 1, :, d:] = dv_own[at, :].astype(BF16)

                @pl.when(c >= s)
                def _():
                    mate_copy(h, s // 2).start()

            else:
                sums[h, s // 2, :, :d] = dk_own[at, :] * inv_root
                sums[h, s // 2, :, d:] = dv_own[at, :]

        @pl.when(h >= 1)
        def _():
            after_mate(h - 1)

        @pl.when(h >= 2)
        def _():
            after_four(h - 2)

        out_copy(h, out_buf, out_hbm, 0).start()
        out_copy(h, dq_buf, dq_hbm, 1).start()
        return carry

    lax.fori_loop(0, kv, head, 0)
    after_mate(kv - 1)
    if kv >= 2:
        after_four(kv - 2)
    after_four(kv - 1)

    acc_k = jnp.zeros((d, tok), F32)
    for h in range(kv):

        @pl.when(c + 2 < n_cp)
        def _():
            front_copy(h, 1).wait_recv()

        both = sums[h, 0] + gz_recv[h, 1].astype(F32)
        dk, dv = both[:, :d], both[:, d:]
        at = slice(h * d, (h + 1) * d)
        dv_ref[:, at] = dv.astype(BF16)
        dkn = unrotate(dk.T, cos_ref[...], sin_ref[...])
        acc_k = acc_k + dkn * k_unit[h]
        dk_ref[:, at] = norm_back(dkn, k_unit[h], k_inv[h, 0:1, :], gk_t[...]).T.astype(BF16)

    part[...] = jnp.concatenate(
        [
            jnp.sum(acc_q[...].T, axis=0, keepdims=True),
            jnp.sum(acc_k.T, axis=0, keepdims=True),
            jnp.zeros((6, d), F32),
        ],
        axis=0,
    )
    dp_recv[a] = part[...]

    def dp_copy(r):
        return pltpu.make_async_remote_copy(
            src_ref=part,
            dst_ref=dp_recv.at[a],
            send_sem=ds_sem.at[r - 1],
            recv_sem=dr_sem.at[r - 1],
            device_id={"dp": lax.rem(a + r, n_dp)},
            device_id_type=MESH,
        )

    def cp_copy(r):
        return pltpu.make_async_remote_copy(
            src_ref=tot,
            dst_ref=cp_recv.at[c],
            send_sem=cs_sem.at[r - 1],
            recv_sem=cr_sem.at[r - 1],
            device_id={"cp": lax.rem(c + r, n_cp)},
            device_id_type=MESH,
        )

    for r in range(1, n_dp):
        dp_copy(r).start()
    for r in range(1, n_dp):
        dp_copy(r).wait_recv()
    total = dp_recv[0]
    for r in range(1, n_dp):
        total = total + dp_recv[r]
    tot[...] = total
    cp_recv[c] = total

    def each(act):
        def step(r, carry):
            act(cp_copy(r))
            return carry

        lax.fori_loop(1, n_cp, step, 0)

    each(lambda copy: copy.start())

    for r in range(1, n_dp):
        kv_copy(r).wait_send()
        dp_copy(r).wait_send()
    for s in range(1, blocks):

        @pl.when(c + s < n_cp)
        def _():
            id_copy(s).wait_send()

    def settle(h, carry):
        for r in range(1, n_dp):
            qg_copy(h, r).wait_send()
        for copy, wanted in ring_plan(h):

            @pl.when(wanted)
            def _():
                copy.wait_send()

        for i in range(2):

            @pl.when(c >= 1 + 2 * i)
            def _():
                mate_copy(h, i).wait_send()

            @pl.when(c >= 4 - 2 * i)
            def _():
                front_copy(h, i).wait_send()

        out_copy(h, out_buf, out_hbm, 0).wait()
        out_copy(h, dq_buf, dq_hbm, 1).wait()
        return carry

    lax.fori_loop(0, kv, settle, 0)
    each(lambda copy: copy.wait())
    total = lax.fori_loop(1, n_cp, lambda r, sofar: sofar + cp_recv[r], cp_recv[0])
    total = total * (1.0 / math.sqrt(tok * n_dp * n_cp))
    gains_ref[...] = total


def hand_out(
    out, dq, dk, dv, gains, out_o, dq_o, dk_o, dv_o, gq_o, gk_o,
    out_v, dq_v, dk_v, dv_v, in_sem, out_sem,
):
    half = out.shape[0] // 2
    plan = [
        (ref.at[at], held.at[at], final.at[at])
        for ref, held, final in ((out, out_v, out_o), (dq, dq_v, dq_o))
        for at in (pl.ds(0, half), pl.ds(half, half))
    ] + [(dk, dk_v, dk_o), (dv, dv_v, dv_o)]
    into = [
        pltpu.make_async_copy(ref, held, in_sem.at[i]) for i, (ref, held, _) in enumerate(plan)
    ]
    away = [
        pltpu.make_async_copy(held, final, out_sem.at[i]) for i, (_, held, final) in enumerate(plan)
    ]
    for copy in into:
        copy.start()
    last = [
        pltpu.make_async_copy(gains.at[0:1], gq_o, out_sem.at[6]),
        pltpu.make_async_copy(gains.at[1:2], gk_o, out_sem.at[7]),
    ]
    for copy in last:
        copy.start()
    for there, copy in zip(into, away):
        there.wait()
        copy.start()
    for copy in away + last:
        copy.wait()


def body(n_dp, n_cp, q_raw, k_raw, values, loss_grad, send_order, doc_blocks, gain_q, gain_k):
    tok, q_width = q_raw.shape
    kw = k_raw.shape[1]
    d = gain_q.shape[0]
    kv = kw // d
    grp = q_width // kw
    blocks = min(MOST_BLK, n_cp)
    reach = blocks - 1
    pair = 4 if grp % 4 == 0 else 1
    assert doc_blocks.shape == (1, 1) and n_cp % 2 == 0 and n_cp >= 6 and MOST_BLK == 5
    frequency = THETA ** (-(np.arange(d // 2, dtype=np.float64) * 2.0 / d))
    angles = frequency[:, None] * np.arange(MOST_BLK * tok, dtype=np.float64)[None, :]
    table = jnp.asarray(np.concatenate([np.cos(angles), np.sin(angles)]).astype(np.float32))
    vmem = pl.BlockSpec(memory_space=pltpu.VMEM)
    hbm = pl.BlockSpec(memory_space=pltpu.HBM)
    anywhere = pl.BlockSpec(memory_space=pl.ANY)
    dma = pltpu.SemaphoreType.DMA
    V = pltpu.VMEM
    outs = pl.pallas_call(
        functools.partial(kernel, n_dp, n_cp, kv, grp, d, tok, pair),
        out_shape=[
            jax.ShapeDtypeStruct((tok, q_width), BF16),
            jax.ShapeDtypeStruct((tok, q_width), BF16),
            jax.ShapeDtypeStruct((tok, kw), BF16),
            jax.ShapeDtypeStruct((tok, kw), BF16),
            jax.ShapeDtypeStruct((8, d), F32),
        ],
        in_specs=[hbm] * 5 + [vmem] + [hbm] * 3,
        out_specs=[anywhere] * 2 + [vmem] * 3,
        scratch_shapes=[
            V((tok, q_width), BF16),
            V((tok, kw), BF16),
            V((tok, kw), BF16),
            V((tok, q_width), BF16),
            V((1, tok), jnp.int32),
            V((1, d), F32),
            V((1, d), F32),
            V(table.shape, F32),
            V((tok, tok), BF16),
            V((tok, 2 * kw), BF16),
            V((tok, 2 * kw), BF16),
            V((kv, tok, 2 * grp * d), BF16),
            V((kv, tok, 2 * grp * d), BF16),
            V((8, 128), jnp.int32),
            V((reach, 8, 128), jnp.int32),
            V((kv, tok, 2 * d), BF16),
            V((kv, reach, tok, 2 * d), BF16),
            V((blocks * tok, d), BF16),
            V((blocks * tok, d), BF16),
            V((d, blocks * tok), BF16),
            V((d, blocks * tok), BF16),
            V((kv, reach, tok, 2 * d), BF16),
            V((kv, 2, tok, 2 * d), BF16),
            V((kv, 2, tok, 2 * d), BF16),
            V((blocks * tok, d), F32),
            V((blocks * tok, d), F32),
            V((kv, 3, tok, 2 * d), F32),
            V((kv, d, tok), F32),
            V((kv, 8, tok), F32),
            V((d // 2, tok), F32),
            V((d // 2, tok), F32),
            V((d, d), F32),
            V((d, d), F32),
            V((tok, tok), F32),
            V((tok, q_width), BF16),
            V((tok, q_width), BF16),
            V((d, tok), F32),
            V((8, d), F32),
            V((8, d), F32),
            V((n_dp, 8, d), F32),
            V((n_cp, 8, d), F32),
            dma((4,)),
            dma((4, kv)),
            dma((2, kv)),
            dma((n_dp - 1,)),
            dma((n_dp - 1,)),
            dma((kv, n_dp - 1)),
            dma((kv, n_dp - 1)),
            dma((reach,)),
            dma((reach,)),
            dma((kv, 4)),
            dma((kv, reach)),
            dma((kv, 2)),
            dma((kv, 2)),
            dma((kv, 2)),
            dma((kv, 2)),
            dma((n_dp - 1,)),
            dma((n_dp - 1,)),
            dma((n_cp - 1,)),
            dma((n_cp - 1,)),
        ],
        compiler_params=pltpu.CompilerParams(
            collective_id=0, has_side_effects=True, vmem_limit_bytes=60 * 1024 * 1024
        ),
    )(
        q_raw, k_raw, values, loss_grad, send_order, doc_blocks,
        gain_q.reshape(1, d), gain_k.reshape(1, d), table,
    )
    outs = pl.pallas_call(
        hand_out,
        out_shape=[jax.ShapeDtypeStruct(x.shape, x.dtype) for x in outs[:4]]
        + [jax.ShapeDtypeStruct((1, d), F32)] * 2,
        in_specs=[anywhere] * 4 + [vmem],
        out_specs=[hbm] * 6,
        scratch_shapes=[V(x.shape, x.dtype) for x in outs[:4]] + [dma((6,)), dma((8,))],
        compiler_params=pltpu.CompilerParams(vmem_limit_bytes=60 * 1024 * 1024),
    )(*outs)
    return (*outs[:4], outs[4].reshape(d), outs[5].reshape(d))


def solution(mesh):
    split = P(("dp", "cp"), None)
    return jax.shard_map(
        functools.partial(body, mesh.shape["dp"], mesh.shape["cp"]),
        mesh=mesh,
        in_specs=(split,) * 5 + (P("dp", "cp"), P(), P()),
        out_specs=(split,) * 4 + (P(), P()),
        check_vma=False,
    )
```

```python
import functools
import math

import jax
import jax.numpy as jnp
import numpy as np
from jax import lax
from jax.experimental import pallas as pl
from jax.experimental.pallas import tpu as pltpu
from jax.sharding import PartitionSpec as P

MOST_BLK = 5
EPSILON = 1e-06
THETA = 1000000.0
NEGATIVE = -1e30
MESH = pl.DeviceIdType.MESH
F32 = jnp.float32
BF16 = jnp.bfloat16


def dot(a, b):
    return jnp.dot(a, b, preferred_element_type=F32)


def dot_nt(a, b):
    return lax.dot_general(a, b, (((1,), (1,)), ((), ())), preferred_element_type=F32)


def flip(x, d):
    parts = [x[:, i : i + d].T for i in range(0, x.shape[1], d)]
    return parts[0] if len(parts) == 1 else jnp.concatenate(parts, axis=1)


def wide(x, n):
    return x if n == 1 else jnp.concatenate([x] * n, axis=1)


def rotate(x, cos, sin):
    half = x.shape[0] // 2
    lead, trail = x[:half], x[half:]
    return jnp.concatenate([lead * cos - trail * sin, trail * cos + lead * sin], axis=0)


def unrotate(x, cos, sin):
    half = x.shape[0] // 2
    lead, trail = x[:half], x[half:]
    return jnp.concatenate([lead * cos + trail * sin, trail * cos - lead * sin], axis=0)


def unit_of(x):
    inv = lax.rsqrt(jnp.mean(x * x, axis=0, keepdims=True) + EPSILON)
    return x * inv, inv


def norm_back(cot, unit, inv, gain):
    scaled = cot * gain
    inner = jnp.mean(scaled * unit, axis=0, keepdims=True)
    return inv * (scaled - unit * inner)


def kernel(
    n_dp, n_cp, kv, grp, d, tok, pair,
    q_hbm, k_hbm, v_hbm, g_hbm, order_hbm, doc_ref, gq_hbm, gk_hbm, table_hbm,
    out_hbm, dq_hbm, dk_ref, dv_ref, gains_ref,
    q_in, k_in, v_in, g_in, order_ref, gq_ref, gk_ref, table_ref, hot, kv_send, kv_recv, qg_send, qg_recv,
    id_send, id_recv, ring_send, ring_recv, keys, vals, keys_t, vals_t,
    grad_send, gy_recv, gz_recv, dk_own, dv_own, sums, held, units, invs, k_unit, k_inv,
    cos_ref, sin_ref, gq_t, gk_t, tri, out_buf, dq_buf, acc_q, part, tot, dp_recv, cp_recv,
    small_sem, in_sem, out_sem, kvs_sem, kvr_sem, qgs_sem, qgr_sem, ids_sem, idr_sem,
    rs_sem, rr_sem, gys_sem, gyr_sem, gzs_sem, gzr_sem, ds_sem, dr_sem, cs_sem, cr_sem,
):
    a = lax.axis_index("dp")
    c = lax.axis_index("cp")
    reach = min(MOST_BLK - 1, n_cp - 1)
    blocks = reach + 1
    per = grp // pair
    shares = kv * per
    early = min(2, kv)
    ahead = min(5, shares)
    span = pair * d
    even = lax.rem(c, 2) == 0
    even_f = even.astype(F32)
    mate = c + 1 - 2 * lax.rem(c, 2)
    width = grp * d
    rows = tok // n_dp
    inv_root = 1.0 / math.sqrt(d)

    def columns(h, size):
        return pl.ds(pl.multiple_of(h * size, size), size)

    def in_copy(h, src, dst, which):
        return pltpu.make_async_copy(
            src.at[:, columns(h, width)], dst.at[:, columns(h, width)], in_sem.at[2 + which, h]
        )

    k_copy = pltpu.make_async_copy(k_hbm, k_in, in_sem.at[0, 0])
    v_copy = pltpu.make_async_copy(v_hbm, v_in, in_sem.at[1, 0])
    small = [
        pltpu.make_async_copy(src, dst, small_sem.at[i])
        for i, (src, dst) in enumerate(
            [(order_hbm, order_ref), (gq_hbm, gq_ref), (gk_hbm, gk_ref), (table_hbm, table_ref)]
        )
    ]
    small[0].start()
    k_copy.start()
    v_copy.start()
    for copy in small[1:]:
        copy.start()
    for h in range(kv):
        in_copy(h, q_hbm, q_in, 0).start()
        in_copy(h, g_hbm, g_in, 1).start()

    barrier = pltpu.get_barrier_semaphore()
    for r in range(1, n_dp):
        pl.semaphore_signal(
            barrier, inc=1, device_id={"dp": lax.rem(a + r, n_dp)}, device_id_type=MESH
        )

    def greet(r, carry):
        pl.semaphore_signal(
            barrier, inc=1, device_id={"cp": lax.rem(c + r, n_cp)}, device_id_type=MESH
        )
        return carry

    lax.fori_loop(1, n_cp, greet, 0)

    own_id = jnp.broadcast_to(doc_ref[...], (8, 128))
    id_send[...] = own_id
    small[0].wait()
    order = jnp.broadcast_to(order_ref[...], (tok, tok)).astype(F32).T
    slot = lax.broadcasted_iota(jnp.int32, (tok, tok), 1)
    hot[...] = jnp.where(order == slot.astype(F32), 1.0, 0.0).astype(BF16)
    small[1].wait()
    small[2].wait()
    gq_t[...] = jnp.broadcast_to(gq_ref[...], (d, d)).T
    gk_t[...] = jnp.broadcast_to(gk_ref[...], (d, d)).T
    tri[...] = jnp.where(
        lax.broadcasted_iota(jnp.int32, (tok, tok), 0)
        <= lax.broadcasted_iota(jnp.int32, (tok, tok), 1),
        0.0,
        NEGATIVE,
    )
    acc_q[...] = jnp.zeros_like(acc_q)
    for s in range(1, blocks):

        @pl.when(c < s)
        def _():
            id_recv[s - 1] = jnp.zeros((8, 128), jnp.int32)
            for h in range(kv):
                ring_recv[h, s - 1] = jnp.zeros((tok, 2 * d), BF16)

    blank = jnp.zeros((tok, 2 * d), BF16)
    for slot_of, missing in (
        ((0, 0), mate < 1),
        ((0, 1), mate < 3),
        ((1, 0), (c + 2 >= n_cp) | (c < 2)),
        ((1, 1), c + 2 >= n_cp),
    ):

        @pl.when(missing)
        def _():
            for h in range(kv):
                (gy_recv if slot_of[0] == 0 else gz_recv)[h, slot_of[1]] = blank

    k_copy.wait()
    v_copy.wait()
    kw = kv * d
    kv_send[:, :kw] = dot(hot[...], k_in[...]).astype(BF16)
    kv_send[:, kw:] = dot(hot[...], v_in[...]).astype(BF16)
    mine = pl.ds(pl.multiple_of(a * rows, rows), rows)
    kv_recv[mine, :] = kv_send[mine, :]

    pl.semaphore_wait(barrier, n_dp - 1 + n_cp - 1)

    def kv_copy(r):
        peer = lax.rem(a + r, n_dp)
        return pltpu.make_async_remote_copy(
            src_ref=kv_send.at[pl.ds(pl.multiple_of(peer * rows, rows), rows), :],
            dst_ref=kv_recv.at[mine, :],
            send_sem=kvs_sem.at[r - 1],
            recv_sem=kvr_sem.at[r - 1],
            device_id={"dp": peer},
            device_id_type=MESH,
        )

    def qg_copy(i, r):
        peer = lax.rem(a + r, n_dp)
        return pltpu.make_async_remote_copy(
            src_ref=qg_send.at[i, pl.ds(pl.multiple_of(peer * rows, rows), rows), :],
            dst_ref=qg_recv.at[i, mine, :],
            send_sem=qgs_sem.at[i, r - 1],
            recv_sem=qgr_sem.at[i, r - 1],
            device_id={"dp": peer},
            device_id_type=MESH,
        )

    def id_copy(s):
        return pltpu.make_async_remote_copy(
            src_ref=id_send,
            dst_ref=id_recv.at[s - 1],
            send_sem=ids_sem.at[s - 1],
            recv_sem=idr_sem.at[s - 1],
            device_id={"cp": lax.rem(c + s, n_cp)},
            device_id_type=MESH,
        )

    def ring_copy(h, src, to, s, kind):
        return pltpu.make_async_remote_copy(
            src_ref=src,
            dst_ref=ring_recv.at[h, s - 1],
            send_sem=rs_sem.at[h, kind],
            recv_sem=rr_sem.at[h, s - 1],
            device_id={"cp": to},
            device_id_type=MESH,
        )

    behind = lax.rem(c + 2, n_cp)
    front = lax.rem(c + n_cp - 2, n_cp)

    def ring_plan(h):
        own, two, four = ring_send.at[h], ring_recv.at[h, 1], ring_recv.at[h, 3]
        return (
            (ring_copy(h, own, behind, 2, 0), c + 2 < n_cp),
            (ring_copy(h, own, mate, 1, 2), even),
            (ring_copy(h, two, behind, 4, 1), (c >= 2) & (c + 2 < n_cp)),
            (ring_copy(h, two, mate, 3, 3), even & (c >= 2)),
            (ring_copy(h, two, mate, 1, 2), jnp.logical_not(even) & (c >= 2)),
            (ring_copy(h, four, mate, 3, 3), jnp.logical_not(even) & (c >= 4)),
        )

    def ring_arrived(h, s):
        @pl.when(c >= s)
        def _():
            ring_copy(h, ring_send.at[h], mate, s, 0).wait_recv()

    def start_if(plan):
        copy, wanted = plan

        @pl.when(wanted)
        def _():
            copy.start()

    def ring_begin(h):
        for plan in ring_plan(h)[:2]:
            start_if(plan)

    def ring_pass(h):
        ring_arrived(h, 2)
        for plan in ring_plan(h)[2:5]:
            start_if(plan)

    def ring_end(h):
        ring_arrived(h, 4)
        start_if(ring_plan(h)[5])

    def mate_copy(h, i):
        return pltpu.make_async_remote_copy(
            src_ref=grad_send.at[h, 2 * i],
            dst_ref=gy_recv.at[h, i],
            send_sem=gys_sem.at[h, i],
            recv_sem=gyr_sem.at[h, i],
            device_id={"cp": mate},
            device_id_type=MESH,
        )

    def front_copy(h, i):
        return pltpu.make_async_remote_copy(
            src_ref=grad_send.at[h, 3 - 2 * i],
            dst_ref=gz_recv.at[h, i],
            send_sem=gzs_sem.at[h, i],
            recv_sem=gzr_sem.at[h, i],
            device_id={"cp": front},
            device_id_type=MESH,
        )

    def after_mate(h):
        for i in range(2):

            @pl.when(mate >= 1 + 2 * i)
            def _():
                mate_copy(h, i).wait_recv()

        one = gy_recv[h, 0].astype(F32)
        three = gy_recv[h, 1].astype(F32)
        sums[h, 0] = sums[h, 0] + one * even_f
        sums[h, 1] = sums[h, 1] + three * even_f + one * (1.0 - even_f)
        grad_send[h, 3] = (sums[h, 2] + three * (1.0 - even_f)).astype(BF16)

        @pl.when(c >= 4)
        def _():
            front_copy(h, 0).start()

    def after_four(h):
        @pl.when((c + 2 < n_cp) & (c >= 2))
        def _():
            front_copy(h, 0).wait_recv()

        grad_send[h, 1] = (sums[h, 1] + gz_recv[h, 0].astype(F32)).astype(BF16)

        @pl.when(c >= 2)
        def _():
            front_copy(h, 1).start()

    for r in range(1, n_dp):
        kv_copy(r).start()
    for s in range(1, blocks):

        @pl.when(c + s < n_cp)
        def _():
            id_copy(s).start()

    def gather(i, carry):
        @pl.when(lax.rem(i, per) == 0)
        def _():
            in_copy(i // per, q_hbm, q_in, 0).wait()
            in_copy(i // per, g_hbm, g_in, 1).wait()

        qg_send[i, :, :span] = dot(hot[...], q_in[:, columns(i, span)]).astype(BF16)
        qg_send[i, :, span:] = dot(hot[...], g_in[:, columns(i, span)]).astype(BF16)
        qg_recv[i, mine, :] = qg_send[i, mine, :]

        @pl.when(i < ahead)
        def _():
            for r in range(1, n_dp):
                qg_copy(i, r).start()

        return carry

    lax.fori_loop(0, shares, gather, 0)

    for s in range(1, blocks):

        @pl.when(c >= s)
        def _():
            id_copy(s).wait_recv()

    before = jnp.zeros((1, 128), F32)
    away = []
    for s in range(1, blocks):
        here = (c >= s).astype(F32)
        same = jnp.where(id_recv[s - 1, 0:1, :] == own_id[0:1, :], here, 0.0)
        before = before + same
        away.append(wide((1.0 - same) * -NEGATIVE, pair))
    small[3].wait()
    half = d // 2
    cos = jnp.zeros((half, tok), F32)
    sin = jnp.zeros((half, tok), F32)
    for s in range(MOST_BLK):
        hit = before == float(s)
        cos = cos + jnp.where(hit, table_ref[:half, s * tok : (s + 1) * tok], 0.0)
        sin = sin + jnp.where(hit, table_ref[half:, s * tok : (s + 1) * tok], 0.0)
    cos_ref[...] = cos
    sin_ref[...] = sin

    for r in range(1, n_dp):
        kv_copy(r).wait_recv()

    for h in range(kv):
        x = kv_recv[:, h * d : (h + 1) * d].astype(F32).T
        unit, inv = unit_of(x)
        k_unit[h] = unit
        k_inv[h] = jnp.broadcast_to(inv, (8, tok))
        turned = rotate(unit * gk_t[...], cos_ref[...], sin_ref[...])
        ring_send[h, :, :d] = turned.T.astype(BF16)
        ring_send[h, :, d:] = kv_recv[:, kw + h * d : kw + (h + 1) * d]
        if h < early:
            ring_begin(h)
    for h in range(early):
        ring_pass(h)
    for h in range(early, kv):
        ring_begin(h)
    for h in range(early):
        ring_end(h)

    def out_copy(h, src, dst, which):
        return pltpu.make_async_copy(
            src.at[:, columns(h, width)], dst.at[:, columns(h, width)], out_sem.at[which, h]
        )

    def head(h, carry):
        ring_arrived(h, 1)
        ring_arrived(h, 3)
        for s in range(blocks):
            both = ring_send[h] if s == 0 else ring_recv[h, s - 1]
            keys[s * tok : (s + 1) * tok, :] = both[:, :d]
            vals[s * tok : (s + 1) * tok, :] = both[:, d:]
            keys_t[:, s * tok : (s + 1) * tok] = both[:, :d].T
            vals_t[:, s * tok : (s + 1) * tok] = both[:, d:].T
        dk_own[...] = jnp.zeros_like(dk_own)
        dv_own[...] = jnp.zeros_like(dv_own)

        def some(j, carry):
            i = h * per + j
            for r in range(1, n_dp):
                qg_copy(i, r).wait_recv()

            @pl.when(i + ahead < shares)
            def _():
                for r in range(1, n_dp):
                    qg_copy(i + ahead, r).start()

            @pl.when(i == 1)
            def _():
                for later in range(early, kv):
                    ring_pass(later)

            cos = wide(cos_ref[...], pair)
            sin = wide(sin_ref[...], pair)
            gain = wide(gq_t[...], pair)
            unit, inv = unit_of(flip(qg_recv[i, :, :span], d).astype(F32))
            units[j] = unit
            invs[j] = jnp.broadcast_to(inv, (8, span))
            turned = rotate(unit * gain, cos, sin).astype(BF16)
            g_rows = qg_recv[i, :, span:]
            g_t = flip(g_rows, d)
            g_rows = jnp.concatenate(
                [g_rows[:, at : at + d] for at in range(0, span, d)], axis=0
            )
            scores = dot(keys[...], turned)
            parts = [scores[s * tok : (s + 1) * tok] for s in range(blocks)]
            parts[0] = parts[0] + wide(tri[...], pair)
            top = jnp.max(parts[0], axis=0, keepdims=True)
            for s in range(1, blocks):
                top = jnp.maximum(top, jnp.max(parts[s], axis=0, keepdims=True) - away[s - 1])
            weights = [
                jnp.exp((parts[s] - (top if s == 0 else top + away[s - 1])) * inv_root)
                for s in range(blocks)
            ]
            weights = jnp.concatenate(weights, axis=0)
            inv_sum = 1.0 / jnp.sum(weights, axis=0, keepdims=True)
            out_t = (dot(vals_t[...], weights.astype(BF16)) * inv_sum).astype(BF16)
            delta = jnp.sum(g_t.astype(F32) * out_t.astype(F32), axis=0, keepdims=True)
            probs = weights * inv_sum
            dprobs = dot(vals[...], g_t)
            dscores = (probs * (dprobs - delta)).astype(BF16)
            dk_own[...] += dot_nt(dscores, turned)
            dv_own[...] += dot(probs.astype(BF16), g_rows)
            held[j] = dscores
            out_buf[:, columns(i, span)] = flip(out_t, d)
            return carry

        lax.fori_loop(0, per, some, 0)
        for s in range(blocks):
            at = slice(s * tok, (s + 1) * tok)
            if s % 2 == 1:
                grad_send[h, s - 1, :, :d] = (dk_own[at, :] * inv_root).astype(BF16)
                grad_send[h, s - 1, :, d:] = dv_own[at, :].astype(BF16)

                @pl.when(c >= s)
                def _():
                    mate_copy(h, s // 2).start()

            else:
                sums[h, s // 2, :, :d] = dk_own[at, :] * inv_root
                sums[h, s // 2, :, d:] = dv_own[at, :]

        @pl.when(h == 0)
        def _():
            for later in range(early, kv):
                ring_end(later)

        def query_grads(j, carry):
            cos = wide(cos_ref[...], pair)
            sin = wide(sin_ref[...], pair)
            unit = units[j]
            dqn = unrotate(dot(keys_t[...], held[j]) * inv_root, cos, sin)
            term = dqn * unit
            acc_q[...] += sum(term[:, at : at + d] for at in range(0, span, d))
            grads = norm_back(dqn, unit, invs[j, 0:1, :], wide(gq_t[...], pair))
            dq_buf[:, columns(h * per + j, span)] = flip(grads.astype(BF16), d)
            return carry

        lax.fori_loop(0, per, query_grads, 0)

        @pl.when(h >= 1)
        def _():
            after_mate(h - 1)

        @pl.when(h >= 2)
        def _():
            after_four(h - 2)

        out_copy(h, out_buf, out_hbm, 0).start()
        out_copy(h, dq_buf, dq_hbm, 1).start()
        return carry

    lax.fori_loop(0, kv, head, 0)
    after_mate(kv - 1)
    if kv >= 2:
        after_four(kv - 2)
    after_four(kv - 1)

    acc_k = jnp.zeros((d, tok), F32)
    for h in range(kv):

        @pl.when(c + 2 < n_cp)
        def _():
            front_copy(h, 1).wait_recv()

        both = sums[h, 0] + gz_recv[h, 1].astype(F32)
        dk, dv = both[:, :d], both[:, d:]
        at = slice(h * d, (h + 1) * d)
        dv_ref[:, at] = dv.astype(BF16)
        dkn = unrotate(dk.T, cos_ref[...], sin_ref[...])
        acc_k = acc_k + dkn * k_unit[h]
        dk_ref[:, at] = norm_back(dkn, k_unit[h], k_inv[h, 0:1, :], gk_t[...]).T.astype(BF16)

    part[...] = jnp.concatenate(
        [
            jnp.sum(acc_q[...].T, axis=0, keepdims=True),
            jnp.sum(acc_k.T, axis=0, keepdims=True),
            jnp.zeros((6, d), F32),
        ],
        axis=0,
    )
    dp_recv[a] = part[...]

    def dp_copy(r):
        return pltpu.make_async_remote_copy(
            src_ref=part,
            dst_ref=dp_recv.at[a],
            send_sem=ds_sem.at[r - 1],
            recv_sem=dr_sem.at[r - 1],
            device_id={"dp": lax.rem(a + r, n_dp)},
            device_id_type=MESH,
        )

    def cp_copy(r):
        return pltpu.make_async_remote_copy(
            src_ref=tot,
            dst_ref=cp_recv.at[c],
            send_sem=cs_sem.at[r - 1],
            recv_sem=cr_sem.at[r - 1],
            device_id={"cp": lax.rem(c + r, n_cp)},
            device_id_type=MESH,
        )

    for r in range(1, n_dp):
        dp_copy(r).start()
    for r in range(1, n_dp):
        dp_copy(r).wait_recv()
    total = dp_recv[0]
    for r in range(1, n_dp):
        total = total + dp_recv[r]
    tot[...] = total
    cp_recv[c] = total

    def each(act):
        def step(r, carry):
            act(cp_copy(r))
            return carry

        lax.fori_loop(1, n_cp, step, 0)

    each(lambda copy: copy.start())

    for r in range(1, n_dp):
        kv_copy(r).wait_send()
        dp_copy(r).wait_send()
    for s in range(1, blocks):

        @pl.when(c + s < n_cp)
        def _():
            id_copy(s).wait_send()

    def settle(h, carry):
        for j in range(per):
            for r in range(1, n_dp):
                qg_copy(h * per + j, r).wait_send()
        for copy, wanted in ring_plan(h):

            @pl.when(wanted)
            def _():
                copy.wait_send()

        for i in range(2):

            @pl.when(c >= 1 + 2 * i)
            def _():
                mate_copy(h, i).wait_send()

            @pl.when(c >= 4 - 2 * i)
            def _():
                front_copy(h, i).wait_send()

        out_copy(h, out_buf, out_hbm, 0).wait()
        out_copy(h, dq_buf, dq_hbm, 1).wait()
        return carry

    lax.fori_loop(0, kv, settle, 0)
    each(lambda copy: copy.wait())
    total = lax.fori_loop(1, n_cp, lambda r, sofar: sofar + cp_recv[r], cp_recv[0])
    total = total * (1.0 / math.sqrt(tok * n_dp * n_cp))
    gains_ref[...] = total


def hand_out(
    out, dq, dk, dv, gains, out_o, dq_o, dk_o, dv_o, gq_o, gk_o,
    out_v, dq_v, dk_v, dv_v, in_sem, out_sem,
):
    half = out.shape[0] // 2
    plan = [
        (ref.at[at], held.at[at], final.at[at])
        for ref, held, final in ((out, out_v, out_o), (dq, dq_v, dq_o))
        for at in (pl.ds(0, half), pl.ds(half, half))
    ] + [(dk, dk_v, dk_o), (dv, dv_v, dv_o)]
    into = [
        pltpu.make_async_copy(ref, held, in_sem.at[i]) for i, (ref, held, _) in enumerate(plan)
    ]
    away = [
        pltpu.make_async_copy(held, final, out_sem.at[i]) for i, (_, held, final) in enumerate(plan)
    ]
    for copy in into:
        copy.start()
    last = [
        pltpu.make_async_copy(gains.at[0:1], gq_o, out_sem.at[6]),
        pltpu.make_async_copy(gains.at[1:2], gk_o, out_sem.at[7]),
    ]
    for copy in last:
        copy.start()
    for there, copy in zip(into, away):
        there.wait()
        copy.start()
    for copy in away + last:
        copy.wait()


def body(n_dp, n_cp, q_raw, k_raw, values, loss_grad, send_order, doc_blocks, gain_q, gain_k):
    tok, q_width = q_raw.shape
    kw = k_raw.shape[1]
    d = gain_q.shape[0]
    kv = kw // d
    grp = q_width // kw
    blocks = min(MOST_BLK, n_cp)
    reach = blocks - 1
    pair = 4 if grp % 8 == 0 else 1
    per = grp // pair
    assert doc_blocks.shape == (1, 1) and n_cp % 2 == 0 and n_cp >= 6 and MOST_BLK == 5
    frequency = THETA ** (-(np.arange(d // 2, dtype=np.float64) * 2.0 / d))
    angles = frequency[:, None] * np.arange(MOST_BLK * tok, dtype=np.float64)[None, :]
    table = jnp.asarray(np.concatenate([np.cos(angles), np.sin(angles)]).astype(np.float32))
    vmem = pl.BlockSpec(memory_space=pltpu.VMEM)
    hbm = pl.BlockSpec(memory_space=pltpu.HBM)
    anywhere = pl.BlockSpec(memory_space=pl.ANY)
    dma = pltpu.SemaphoreType.DMA
    V = pltpu.VMEM
    outs = pl.pallas_call(
        functools.partial(kernel, n_dp, n_cp, kv, grp, d, tok, pair),
        out_shape=[
            jax.ShapeDtypeStruct((tok, q_width), BF16),
            jax.ShapeDtypeStruct((tok, q_width), BF16),
            jax.ShapeDtypeStruct((tok, kw), BF16),
            jax.ShapeDtypeStruct((tok, kw), BF16),
            jax.ShapeDtypeStruct((8, d), F32),
        ],
        in_specs=[hbm] * 5 + [vmem] + [hbm] * 3,
        out_specs=[anywhere] * 2 + [vmem] * 3,
        scratch_shapes=[
            V((tok, q_width), BF16),
            V((tok, kw), BF16),
            V((tok, kw), BF16),
            V((tok, q_width), BF16),
            V((1, tok), jnp.int32),
            V((1, d), F32),
            V((1, d), F32),
            V(table.shape, F32),
            V((tok, tok), BF16),
            V((tok, 2 * kw), BF16),
            V((tok, 2 * kw), BF16),
            V((kv * per, tok, 2 * pair * d), BF16),
            V((kv * per, tok, 2 * pair * d), BF16),
            V((8, 128), jnp.int32),
            V((reach, 8, 128), jnp.int32),
            V((kv, tok, 2 * d), BF16),
            V((kv, reach, tok, 2 * d), BF16),
            V((blocks * tok, d), BF16),
            V((blocks * tok, d), BF16),
            V((d, blocks * tok), BF16),
            V((d, blocks * tok), BF16),
            V((kv, reach, tok, 2 * d), BF16),
            V((kv, 2, tok, 2 * d), BF16),
            V((kv, 2, tok, 2 * d), BF16),
            V((blocks * tok, d), F32),
            V((blocks * tok, d), F32),
            V((kv, 3, tok, 2 * d), F32),
            V((per, blocks * tok, pair * d), BF16),
            V((per, d, pair * d), F32),
            V((per, 8, pair * d), F32),
            V((kv, d, tok), F32),
            V((kv, 8, tok), F32),
            V((d // 2, tok), F32),
            V((d // 2, tok), F32),
            V((d, d), F32),
            V((d, d), F32),
            V((tok, tok), F32),
            V((tok, q_width), BF16),
            V((tok, q_width), BF16),
            V((d, tok), F32),
            V((8, d), F32),
            V((8, d), F32),
            V((n_dp, 8, d), F32),
            V((n_cp, 8, d), F32),
            dma((4,)),
            dma((4, kv)),
            dma((2, kv)),
            dma((n_dp - 1,)),
            dma((n_dp - 1,)),
            dma((kv * per, n_dp - 1)),
            dma((kv * per, n_dp - 1)),
            dma((reach,)),
            dma((reach,)),
            dma((kv, 4)),
            dma((kv, reach)),
            dma((kv, 2)),
            dma((kv, 2)),
            dma((kv, 2)),
            dma((kv, 2)),
            dma((n_dp - 1,)),
            dma((n_dp - 1,)),
            dma((n_cp - 1,)),
            dma((n_cp - 1,)),
        ],
        compiler_params=pltpu.CompilerParams(
            collective_id=0, has_side_effects=True, vmem_limit_bytes=60 * 1024 * 1024
        ),
    )(
        q_raw, k_raw, values, loss_grad, send_order, doc_blocks,
        gain_q.reshape(1, d), gain_k.reshape(1, d), table,
    )
    outs = pl.pallas_call(
        hand_out,
        out_shape=[jax.ShapeDtypeStruct(x.shape, x.dtype) for x in outs[:4]]
        + [jax.ShapeDtypeStruct((1, d), F32)] * 2,
        in_specs=[anywhere] * 4 + [vmem],
        out_specs=[hbm] * 6,
        scratch_shapes=[V(x.shape, x.dtype) for x in outs[:4]] + [dma((6,)), dma((8,))],
        compiler_params=pltpu.CompilerParams(vmem_limit_bytes=60 * 1024 * 1024),
    )(*outs)
    return (*outs[:4], outs[4].reshape(d), outs[5].reshape(d))


def solution(mesh):
    split = P(("dp", "cp"), None)
    return jax.shard_map(
        functools.partial(body, mesh.shape["dp"], mesh.shape["cp"]),
        mesh=mesh,
        in_specs=(split,) * 5 + (P("dp", "cp"), P(), P()),
        out_specs=(split,) * 4 + (P(), P()),
        check_vma=False,
    )
```

```python
import functools
import math

import jax
import jax.numpy as jnp
import numpy as np
from jax import lax
from jax.experimental import pallas as pl
from jax.experimental.pallas import tpu as pltpu
from jax.sharding import PartitionSpec as P

MOST_BLK = 5
EPSILON = 1e-06
THETA = 1000000.0
NEGATIVE = -1e30
MESH = pl.DeviceIdType.MESH
F32 = jnp.float32
BF16 = jnp.bfloat16


def dot(a, b):
    return jnp.dot(a, b, preferred_element_type=F32)


def dot_nt(a, b):
    return lax.dot_general(a, b, (((1,), (1,)), ((), ())), preferred_element_type=F32)


def flip(x, d):
    parts = [x[:, i : i + d].T for i in range(0, x.shape[1], d)]
    return parts[0] if len(parts) == 1 else jnp.concatenate(parts, axis=1)


def wide(x, n):
    return x if n == 1 else jnp.concatenate([x] * n, axis=1)


def rotate(x, cos, sin):
    half = x.shape[0] // 2
    lead, trail = x[:half], x[half:]
    return jnp.concatenate([lead * cos - trail * sin, trail * cos + lead * sin], axis=0)


def unrotate(x, cos, sin):
    half = x.shape[0] // 2
    lead, trail = x[:half], x[half:]
    return jnp.concatenate([lead * cos + trail * sin, trail * cos - lead * sin], axis=0)


def unit_of(x):
    inv = lax.rsqrt(jnp.mean(x * x, axis=0, keepdims=True) + EPSILON)
    return x * inv, inv


def norm_back(cot, unit, inv, gain):
    scaled = cot * gain
    inner = jnp.mean(scaled * unit, axis=0, keepdims=True)
    return inv * (scaled - unit * inner)


def kernel(
    n_dp, n_cp, kv, grp, d, tok, pair,
    q_hbm, k_hbm, v_hbm, g_hbm, order_hbm, doc_ref, gq_hbm, gk_hbm, table_hbm,
    out_buf, dq_buf, dk_ref, dv_ref, gains_ref,
    q_in, k_in, v_in, g_in, order_ref, gq_ref, gk_ref, table_ref, hot, kv_send, kv_recv, qg_send, qg_recv,
    id_send, id_recv, ring_send, ring_recv, keys, vals, keys_t, vals_t,
    grad_send, gy_recv, gz_recv, dk_own, dv_own, sums, held, units, invs, k_unit, k_inv,
    cos_ref, sin_ref, gq_t, gk_t, tri, acc_q, part, tot, dp_recv, cp_recv,
    small_sem, in_sem, kvs_sem, kvr_sem, qgs_sem, qgr_sem, ids_sem, idr_sem,
    rs_sem, rr_sem, gys_sem, gyr_sem, gzs_sem, gzr_sem, ds_sem, dr_sem, cs_sem, cr_sem,
):
    a = lax.axis_index("dp")
    c = lax.axis_index("cp")
    reach = min(MOST_BLK - 1, n_cp - 1)
    blocks = reach + 1
    per = grp // pair
    shares = kv * per
    early = min(2, kv)
    ahead = min(5, shares)
    span = pair * d
    even = lax.rem(c, 2) == 0
    even_f = even.astype(F32)
    mate = c + 1 - 2 * lax.rem(c, 2)
    width = grp * d
    rows = tok // n_dp
    inv_root = 1.0 / math.sqrt(d)

    def columns(h, size):
        return pl.ds(pl.multiple_of(h * size, size), size)

    def in_copy(h, src, dst, which):
        return pltpu.make_async_copy(
            src.at[:, columns(h, width)], dst.at[:, columns(h, width)], in_sem.at[2 + which, h]
        )

    k_copy = pltpu.make_async_copy(k_hbm, k_in, in_sem.at[0, 0])
    v_copy = pltpu.make_async_copy(v_hbm, v_in, in_sem.at[1, 0])
    small = [
        pltpu.make_async_copy(src, dst, small_sem.at[i])
        for i, (src, dst) in enumerate(
            [(order_hbm, order_ref), (gq_hbm, gq_ref), (gk_hbm, gk_ref), (table_hbm, table_ref)]
        )
    ]
    small[0].start()
    k_copy.start()
    v_copy.start()
    for copy in small[1:]:
        copy.start()
    for h in range(kv):
        in_copy(h, q_hbm, q_in, 0).start()
        in_copy(h, g_hbm, g_in, 1).start()

    barrier = pltpu.get_barrier_semaphore()
    for r in range(1, n_dp):
        pl.semaphore_signal(
            barrier, inc=1, device_id={"dp": lax.rem(a + r, n_dp)}, device_id_type=MESH
        )

    def greet(r, carry):
        pl.semaphore_signal(
            barrier, inc=1, device_id={"cp": lax.rem(c + r, n_cp)}, device_id_type=MESH
        )
        return carry

    lax.fori_loop(1, n_cp, greet, 0)

    own_id = jnp.broadcast_to(doc_ref[...], (8, 128))
    id_send[...] = own_id
    small[0].wait()
    order = jnp.broadcast_to(order_ref[...], (tok, tok)).astype(F32).T
    slot = lax.broadcasted_iota(jnp.int32, (tok, tok), 1)
    hot[...] = jnp.where(order == slot.astype(F32), 1.0, 0.0).astype(BF16)
    small[1].wait()
    small[2].wait()
    gq_t[...] = jnp.broadcast_to(gq_ref[...], (d, d)).T
    gk_t[...] = jnp.broadcast_to(gk_ref[...], (d, d)).T
    tri[...] = jnp.where(
        lax.broadcasted_iota(jnp.int32, (tok, tok), 0)
        <= lax.broadcasted_iota(jnp.int32, (tok, tok), 1),
        0.0,
        NEGATIVE,
    )
    acc_q[...] = jnp.zeros_like(acc_q)
    for s in range(1, blocks):

        @pl.when(c < s)
        def _():
            id_recv[s - 1] = jnp.zeros((8, 128), jnp.int32)
            for h in range(kv):
                ring_recv[h, s - 1] = jnp.zeros((tok, 2 * d), BF16)

    blank = jnp.zeros((tok, 2 * d), BF16)
    for slot_of, missing in (
        ((0, 0), mate < 1),
        ((0, 1), mate < 3),
        ((1, 0), (c + 2 >= n_cp) | (c < 2)),
        ((1, 1), c + 2 >= n_cp),
    ):

        @pl.when(missing)
        def _():
            for h in range(kv):
                (gy_recv if slot_of[0] == 0 else gz_recv)[h, slot_of[1]] = blank

    k_copy.wait()
    v_copy.wait()
    kw = kv * d
    kv_send[:, :kw] = dot(hot[...], k_in[...]).astype(BF16)
    kv_send[:, kw:] = dot(hot[...], v_in[...]).astype(BF16)
    mine = pl.ds(pl.multiple_of(a * rows, rows), rows)
    kv_recv[mine, :] = kv_send[mine, :]

    pl.semaphore_wait(barrier, n_dp - 1 + n_cp - 1)

    def kv_copy(r):
        peer = lax.rem(a + r, n_dp)
        return pltpu.make_async_remote_copy(
            src_ref=kv_send.at[pl.ds(pl.multiple_of(peer * rows, rows), rows), :],
            dst_ref=kv_recv.at[mine, :],
            send_sem=kvs_sem.at[r - 1],
            recv_sem=kvr_sem.at[r - 1],
            device_id={"dp": peer},
            device_id_type=MESH,
        )

    def qg_copy(i, r):
        peer = lax.rem(a + r, n_dp)
        return pltpu.make_async_remote_copy(
            src_ref=qg_send.at[i, pl.ds(pl.multiple_of(peer * rows, rows), rows), :],
            dst_ref=qg_recv.at[i, mine, :],
            send_sem=qgs_sem.at[i, r - 1],
            recv_sem=qgr_sem.at[i, r - 1],
            device_id={"dp": peer},
            device_id_type=MESH,
        )

    def id_copy(s):
        return pltpu.make_async_remote_copy(
            src_ref=id_send,
            dst_ref=id_recv.at[s - 1],
            send_sem=ids_sem.at[s - 1],
            recv_sem=idr_sem.at[s - 1],
            device_id={"cp": lax.rem(c + s, n_cp)},
            device_id_type=MESH,
        )

    def ring_copy(h, src, to, s, kind):
        return pltpu.make_async_remote_copy(
            src_ref=src,
            dst_ref=ring_recv.at[h, s - 1],
            send_sem=rs_sem.at[h, kind],
            recv_sem=rr_sem.at[h, s - 1],
            device_id={"cp": to},
            device_id_type=MESH,
        )

    behind = lax.rem(c + 2, n_cp)
    front = lax.rem(c + n_cp - 2, n_cp)

    def ring_plan(h):
        own, two, four = ring_send.at[h], ring_recv.at[h, 1], ring_recv.at[h, 3]
        return (
            (ring_copy(h, own, behind, 2, 0), c + 2 < n_cp),
            (ring_copy(h, own, mate, 1, 2), even),
            (ring_copy(h, two, behind, 4, 1), (c >= 2) & (c + 2 < n_cp)),
            (ring_copy(h, two, mate, 3, 3), even & (c >= 2)),
            (ring_copy(h, two, mate, 1, 2), jnp.logical_not(even) & (c >= 2)),
            (ring_copy(h, four, mate, 3, 3), jnp.logical_not(even) & (c >= 4)),
        )

    def ring_arrived(h, s):
        @pl.when(c >= s)
        def _():
            ring_copy(h, ring_send.at[h], mate, s, 0).wait_recv()

    def start_if(plan):
        copy, wanted = plan

        @pl.when(wanted)
        def _():
            copy.start()

    def ring_begin(h):
        for plan in ring_plan(h)[:2]:
            start_if(plan)

    def ring_pass(h):
        ring_arrived(h, 2)
        for plan in ring_plan(h)[2:5]:
            start_if(plan)

    def ring_end(h):
        ring_arrived(h, 4)
        start_if(ring_plan(h)[5])

    def mate_copy(h, i):
        return pltpu.make_async_remote_copy(
            src_ref=grad_send.at[h, 2 * i],
            dst_ref=gy_recv.at[h, i],
            send_sem=gys_sem.at[h, i],
            recv_sem=gyr_sem.at[h, i],
            device_id={"cp": mate},
            device_id_type=MESH,
        )

    def front_copy(h, i):
        return pltpu.make_async_remote_copy(
            src_ref=grad_send.at[h, 3 - 2 * i],
            dst_ref=gz_recv.at[h, i],
            send_sem=gzs_sem.at[h, i],
            recv_sem=gzr_sem.at[h, i],
            device_id={"cp": front},
            device_id_type=MESH,
        )

    def after_mate(h):
        for i in range(2):

            @pl.when(mate >= 1 + 2 * i)
            def _():
                mate_copy(h, i).wait_recv()

        one = gy_recv[h, 0].astype(F32)
        three = gy_recv[h, 1].astype(F32)
        sums[h, 0] = sums[h, 0] + one * even_f
        sums[h, 1] = sums[h, 1] + three * even_f + one * (1.0 - even_f)
        grad_send[h, 3] = (sums[h, 2] + three * (1.0 - even_f)).astype(BF16)

        @pl.when(c >= 4)
        def _():
            front_copy(h, 0).start()

    def after_four(h):
        @pl.when((c + 2 < n_cp) & (c >= 2))
        def _():
            front_copy(h, 0).wait_recv()

        grad_send[h, 1] = (sums[h, 1] + gz_recv[h, 0].astype(F32)).astype(BF16)

        @pl.when(c >= 2)
        def _():
            front_copy(h, 1).start()

    for r in range(1, n_dp):
        kv_copy(r).start()
    for s in range(1, blocks):

        @pl.when(c + s < n_cp)
        def _():
            id_copy(s).start()

    def gather(i, carry):
        @pl.when(lax.rem(i, per) == 0)
        def _():
            in_copy(i // per, q_hbm, q_in, 0).wait()
            in_copy(i // per, g_hbm, g_in, 1).wait()

        qg_send[i, :, :span] = dot(hot[...], q_in[:, columns(i, span)]).astype(BF16)
        qg_send[i, :, span:] = dot(hot[...], g_in[:, columns(i, span)]).astype(BF16)
        qg_recv[i, mine, :] = qg_send[i, mine, :]

        @pl.when(i < ahead)
        def _():
            for r in range(1, n_dp):
                qg_copy(i, r).start()

        return carry

    lax.fori_loop(0, shares, gather, 0)

    for s in range(1, blocks):

        @pl.when(c >= s)
        def _():
            id_copy(s).wait_recv()

    before = jnp.zeros((1, 128), F32)
    away = []
    for s in range(1, blocks):
        here = (c >= s).astype(F32)
        same = jnp.where(id_recv[s - 1, 0:1, :] == own_id[0:1, :], here, 0.0)
        before = before + same
        away.append(wide((1.0 - same) * -NEGATIVE, pair))
    small[3].wait()
    half = d // 2
    cos = jnp.zeros((half, tok), F32)
    sin = jnp.zeros((half, tok), F32)
    for s in range(MOST_BLK):
        hit = before == float(s)
        cos = cos + jnp.where(hit, table_ref[:half, s * tok : (s + 1) * tok], 0.0)
        sin = sin + jnp.where(hit, table_ref[half:, s * tok : (s + 1) * tok], 0.0)
    cos_ref[...] = cos
    sin_ref[...] = sin

    for r in range(1, n_dp):
        kv_copy(r).wait_recv()

    for h in range(kv):
        x = kv_recv[:, h * d : (h + 1) * d].astype(F32).T
        unit, inv = unit_of(x)
        k_unit[h] = unit
        k_inv[h] = jnp.broadcast_to(inv, (8, tok))
        turned = rotate(unit * gk_t[...], cos_ref[...], sin_ref[...])
        ring_send[h, :, :d] = turned.T.astype(BF16)
        ring_send[h, :, d:] = kv_recv[:, kw + h * d : kw + (h + 1) * d]
        if h < early:
            ring_begin(h)
    for h in range(early):
        ring_pass(h)
    for h in range(early, kv):
        ring_begin(h)
    for h in range(early):
        ring_end(h)

    def head(h, carry):
        ring_arrived(h, 1)
        ring_arrived(h, 3)
        for s in range(blocks):
            both = ring_send[h] if s == 0 else ring_recv[h, s - 1]
            keys[s * tok : (s + 1) * tok, :] = both[:, :d]
            vals[s * tok : (s + 1) * tok, :] = both[:, d:]
            keys_t[:, s * tok : (s + 1) * tok] = both[:, :d].T
            vals_t[:, s * tok : (s + 1) * tok] = both[:, d:].T
        dk_own[...] = jnp.zeros_like(dk_own)
        dv_own[...] = jnp.zeros_like(dv_own)

        def some(j, carry):
            i = h * per + j
            for r in range(1, n_dp):
                qg_copy(i, r).wait_recv()

            @pl.when(i + ahead < shares)
            def _():
                for r in range(1, n_dp):
                    qg_copy(i + ahead, r).start()

            @pl.when(i == 1)
            def _():
                for later in range(early, kv):
                    ring_pass(later)

            cos = wide(cos_ref[...], pair)
            sin = wide(sin_ref[...], pair)
            gain = wide(gq_t[...], pair)
            unit, inv = unit_of(flip(qg_recv[i, :, :span], d).astype(F32))
            units[j] = unit
            invs[j] = jnp.broadcast_to(inv, (8, span))
            turned = rotate(unit * gain, cos, sin).astype(BF16)
            g_rows = qg_recv[i, :, span:]
            g_t = flip(g_rows, d)
            g_rows = jnp.concatenate(
                [g_rows[:, at : at + d] for at in range(0, span, d)], axis=0
            )
            scores = dot(keys[...], turned)
            parts = [scores[s * tok : (s + 1) * tok] for s in range(blocks)]
            parts[0] = parts[0] + wide(tri[...], pair)
            top = jnp.max(parts[0], axis=0, keepdims=True)
            for s in range(1, blocks):
                top = jnp.maximum(top, jnp.max(parts[s], axis=0, keepdims=True) - away[s - 1])
            weights = [
                jnp.exp((parts[s] - (top if s == 0 else top + away[s - 1])) * inv_root)
                for s in range(blocks)
            ]
            weights = jnp.concatenate(weights, axis=0)
            inv_sum = 1.0 / jnp.sum(weights, axis=0, keepdims=True)
            out_t = (dot(vals_t[...], weights.astype(BF16)) * inv_sum).astype(BF16)
            delta = jnp.sum(g_t.astype(F32) * out_t.astype(F32), axis=0, keepdims=True)
            probs = weights * inv_sum
            dprobs = dot(vals[...], g_t)
            dscores = (probs * (dprobs - delta)).astype(BF16)
            dk_own[...] += dot_nt(dscores, turned)
            dv_own[...] += dot(probs.astype(BF16), g_rows)
            held[j] = dscores
            out_buf[:, columns(i, span)] = flip(out_t, d)
            return carry

        lax.fori_loop(0, per, some, 0)
        for s in range(blocks):
            at = slice(s * tok, (s + 1) * tok)
            if s % 2 == 1:
                grad_send[h, s - 1, :, :d] = (dk_own[at, :] * inv_root).astype(BF16)
                grad_send[h, s - 1, :, d:] = dv_own[at, :].astype(BF16)

                @pl.when(c >= s)
                def _():
                    mate_copy(h, s // 2).start()

            else:
                sums[h, s // 2, :, :d] = dk_own[at, :] * inv_root
                sums[h, s // 2, :, d:] = dv_own[at, :]

        @pl.when(h == 0)
        def _():
            for later in range(early, kv):
                ring_end(later)

        def query_grads(j, carry):
            cos = wide(cos_ref[...], pair)
            sin = wide(sin_ref[...], pair)
            unit = units[j]
            dqn = unrotate(dot(keys_t[...], held[j]) * inv_root, cos, sin)
            term = dqn * unit
            acc_q[...] += sum(term[:, at : at + d] for at in range(0, span, d))
            grads = norm_back(dqn, unit, invs[j, 0:1, :], wide(gq_t[...], pair))
            dq_buf[:, columns(h * per + j, span)] = flip(grads.astype(BF16), d)
            return carry

        lax.fori_loop(0, per, query_grads, 0)

        @pl.when(h >= 1)
        def _():
            after_mate(h - 1)

        @pl.when(h >= 2)
        def _():
            after_four(h - 2)

        return carry

    lax.fori_loop(0, kv, head, 0)
    after_mate(kv - 1)
    if kv >= 2:
        after_four(kv - 2)
    acc_k = jnp.zeros((d, tok), F32)
    for h in range(kv):
        if h == max(kv - 2, 0):
            after_four(kv - 1)

        @pl.when(c + 2 < n_cp)
        def _():
            front_copy(h, 1).wait_recv()

        both = sums[h, 0] + gz_recv[h, 1].astype(F32)
        dk, dv = both[:, :d], both[:, d:]
        at = slice(h * d, (h + 1) * d)
        dv_ref[:, at] = dv.astype(BF16)
        dkn = unrotate(dk.T, cos_ref[...], sin_ref[...])
        acc_k = acc_k + dkn * k_unit[h]
        dk_ref[:, at] = norm_back(dkn, k_unit[h], k_inv[h, 0:1, :], gk_t[...]).T.astype(BF16)

    part[...] = jnp.concatenate(
        [
            jnp.sum(acc_q[...].T, axis=0, keepdims=True),
            jnp.sum(acc_k.T, axis=0, keepdims=True),
            jnp.zeros((6, d), F32),
        ],
        axis=0,
    )
    dp_recv[a] = part[...]

    def dp_copy(r):
        return pltpu.make_async_remote_copy(
            src_ref=part,
            dst_ref=dp_recv.at[a],
            send_sem=ds_sem.at[r - 1],
            recv_sem=dr_sem.at[r - 1],
            device_id={"dp": lax.rem(a + r, n_dp)},
            device_id_type=MESH,
        )

    def cp_copy(r):
        return pltpu.make_async_remote_copy(
            src_ref=tot,
            dst_ref=cp_recv.at[c],
            send_sem=cs_sem.at[r - 1],
            recv_sem=cr_sem.at[r - 1],
            device_id={"cp": lax.rem(c + r, n_cp)},
            device_id_type=MESH,
        )

    for r in range(1, n_dp):
        dp_copy(r).start()
    for r in range(1, n_dp):
        dp_copy(r).wait_recv()
    total = dp_recv[0]
    for r in range(1, n_dp):
        total = total + dp_recv[r]
    tot[...] = total
    cp_recv[c] = total

    def each(act):
        def step(r, carry):
            act(cp_copy(r))
            return carry

        lax.fori_loop(1, n_cp, step, 0)

    each(lambda copy: copy.start())

    for r in range(1, n_dp):
        kv_copy(r).wait_send()
        dp_copy(r).wait_send()
    for s in range(1, blocks):

        @pl.when(c + s < n_cp)
        def _():
            id_copy(s).wait_send()

    def settle(h, carry):
        for j in range(per):
            for r in range(1, n_dp):
                qg_copy(h * per + j, r).wait_send()
        for copy, wanted in ring_plan(h):

            @pl.when(wanted)
            def _():
                copy.wait_send()

        for i in range(2):

            @pl.when(c >= 1 + 2 * i)
            def _():
                mate_copy(h, i).wait_send()

            @pl.when(c >= 4 - 2 * i)
            def _():
                front_copy(h, i).wait_send()

        return carry

    lax.fori_loop(0, kv, settle, 0)
    each(lambda copy: copy.wait())
    total = lax.fori_loop(1, n_cp, lambda r, sofar: sofar + cp_recv[r], cp_recv[0])
    total = total * (1.0 / math.sqrt(tok * n_dp * n_cp))
    gains_ref[...] = total


def hand_out(out, dq, dk, dv, gains, out_o, dq_o, dk_o, dv_o, gq_o, gk_o, sem):
    pairs = [
        (out, out_o), (dq, dq_o), (dk, dk_o), (dv, dv_o),
        (gains.at[0:1], gq_o), (gains.at[1:2], gk_o),
    ]
    copies = [pltpu.make_async_copy(src, dst, sem.at[i]) for i, (src, dst) in enumerate(pairs)]
    for copy in copies:
        copy.start()
    for copy in copies:
        copy.wait()


def body(n_dp, n_cp, q_raw, k_raw, values, loss_grad, send_order, doc_blocks, gain_q, gain_k):
    tok, q_width = q_raw.shape
    kw = k_raw.shape[1]
    d = gain_q.shape[0]
    kv = kw // d
    grp = q_width // kw
    blocks = min(MOST_BLK, n_cp)
    reach = blocks - 1
    pair = 4 if grp % 8 == 0 else 1
    per = grp // pair
    assert doc_blocks.shape == (1, 1) and n_cp % 2 == 0 and n_cp >= 6 and MOST_BLK == 5
    frequency = THETA ** (-(np.arange(d // 2, dtype=np.float64) * 2.0 / d))
    angles = frequency[:, None] * np.arange(MOST_BLK * tok, dtype=np.float64)[None, :]
    table = jnp.asarray(np.concatenate([np.cos(angles), np.sin(angles)]).astype(np.float32))
    vmem = pl.BlockSpec(memory_space=pltpu.VMEM)
    hbm = pl.BlockSpec(memory_space=pltpu.HBM)
    dma = pltpu.SemaphoreType.DMA
    V = pltpu.VMEM
    outs = pl.pallas_call(
        functools.partial(kernel, n_dp, n_cp, kv, grp, d, tok, pair),
        out_shape=[
            V((tok, q_width), BF16),
            V((tok, q_width), BF16),
            V((tok, kw), BF16),
            V((tok, kw), BF16),
            V((8, d), F32),
        ],
        in_specs=[hbm] * 5 + [vmem] + [hbm] * 3,
        out_specs=[vmem] * 5,
        scratch_shapes=[
            V((tok, q_width), BF16),
            V((tok, kw), BF16),
            V((tok, kw), BF16),
            V((tok, q_width), BF16),
            V((1, tok), jnp.int32),
            V((1, d), F32),
            V((1, d), F32),
            V(table.shape, F32),
            V((tok, tok), BF16),
            V((tok, 2 * kw), BF16),
            V((tok, 2 * kw), BF16),
            V((kv * per, tok, 2 * pair * d), BF16),
            V((kv * per, tok, 2 * pair * d), BF16),
            V((8, 128), jnp.int32),
            V((reach, 8, 128), jnp.int32),
            V((kv, tok, 2 * d), BF16),
            V((kv, reach, tok, 2 * d), BF16),
            V((blocks * tok, d), BF16),
            V((blocks * tok, d), BF16),
            V((d, blocks * tok), BF16),
            V((d, blocks * tok), BF16),
            V((kv, reach, tok, 2 * d), BF16),
            V((kv, 2, tok, 2 * d), BF16),
            V((kv, 2, tok, 2 * d), BF16),
            V((blocks * tok, d), F32),
            V((blocks * tok, d), F32),
            V((kv, 3, tok, 2 * d), F32),
            V((per, blocks * tok, pair * d), BF16),
            V((per, d, pair * d), F32),
            V((per, 8, pair * d), F32),
            V((kv, d, tok), F32),
            V((kv, 8, tok), F32),
            V((d // 2, tok), F32),
            V((d // 2, tok), F32),
            V((d, d), F32),
            V((d, d), F32),
            V((tok, tok), F32),
            V((d, tok), F32),
            V((8, d), F32),
            V((8, d), F32),
            V((n_dp, 8, d), F32),
            V((n_cp, 8, d), F32),
            dma((4,)),
            dma((4, kv)),
            dma((n_dp - 1,)),
            dma((n_dp - 1,)),
            dma((kv * per, n_dp - 1)),
            dma((kv * per, n_dp - 1)),
            dma((reach,)),
            dma((reach,)),
            dma((kv, 4)),
            dma((kv, reach)),
            dma((kv, 2)),
            dma((kv, 2)),
            dma((kv, 2)),
            dma((kv, 2)),
            dma((n_dp - 1,)),
            dma((n_dp - 1,)),
            dma((n_cp - 1,)),
            dma((n_cp - 1,)),
        ],
        compiler_params=pltpu.CompilerParams(
            collective_id=0, has_side_effects=True, vmem_limit_bytes=56 * 1024 * 1024
        ),
    )(
        q_raw, k_raw, values, loss_grad, send_order, doc_blocks,
        gain_q.reshape(1, d), gain_k.reshape(1, d), table,
    )
    outs = pl.pallas_call(
        hand_out,
        out_shape=[jax.ShapeDtypeStruct(x.shape, x.dtype) for x in outs[:4]]
        + [jax.ShapeDtypeStruct((1, d), F32)] * 2,
        in_specs=[vmem] * 5,
        out_specs=[hbm] * 6,
        scratch_shapes=[dma((6,))],
        compiler_params=pltpu.CompilerParams(vmem_limit_bytes=8 * 1024 * 1024),
    )(*outs)
    return (*outs[:4], outs[4].reshape(d), outs[5].reshape(d))


def solution(mesh):
    split = P(("dp", "cp"), None)
    return jax.shard_map(
        functools.partial(body, mesh.shape["dp"], mesh.shape["cp"]),
        mesh=mesh,
        in_specs=(split,) * 5 + (P("dp", "cp"), P(), P()),
        out_specs=(split,) * 4 + (P(), P()),
        check_vma=False,
    )
```

```python
import functools
import math

import jax
import jax.numpy as jnp
import numpy as np
from jax import lax
from jax.experimental import pallas as pl
from jax.experimental.pallas import tpu as pltpu
from jax.sharding import PartitionSpec as P

MOST_BLK = 5
EPSILON = 1e-06
THETA = 1000000.0
NEGATIVE = -1e30
MESH = pl.DeviceIdType.MESH
F32 = jnp.float32
BF16 = jnp.bfloat16


def dot(a, b):
    return jnp.dot(a, b, preferred_element_type=F32)


def dot_nt(a, b):
    return lax.dot_general(a, b, (((1,), (1,)), ((), ())), preferred_element_type=F32)


def flip(x, d):
    parts = [x[:, i : i + d].T for i in range(0, x.shape[1], d)]
    return parts[0] if len(parts) == 1 else jnp.concatenate(parts, axis=1)


def wide(x, n):
    return x if n == 1 else jnp.concatenate([x] * n, axis=1)


def rotate(x, cos, sin):
    half = x.shape[0] // 2
    lead, trail = x[:half], x[half:]
    return jnp.concatenate([lead * cos - trail * sin, trail * cos + lead * sin], axis=0)


def unrotate(x, cos, sin):
    half = x.shape[0] // 2
    lead, trail = x[:half], x[half:]
    return jnp.concatenate([lead * cos + trail * sin, trail * cos - lead * sin], axis=0)


def unit_of(x):
    inv = lax.rsqrt(jnp.mean(x * x, axis=0, keepdims=True) + EPSILON)
    return x * inv, inv


def norm_back(cot, unit, inv, gain):
    scaled = cot * gain
    inner = jnp.mean(scaled * unit, axis=0, keepdims=True)
    return inv * (scaled - unit * inner)


def kernel(
    n_dp, n_cp, kv, grp, d, tok, pair,
    q_hbm, k_hbm, v_hbm, g_hbm, order_hbm, doc_ref, gq_hbm, gk_hbm, table_hbm,
    out_buf, dq_buf, dk_ref, dv_ref, gains_ref,
    q_in, k_in, v_in, g_in, order_ref, gq_ref, gk_ref, table_ref, hot, kv_send, kv_recv, qg_send, qg_recv,
    id_send, id_recv, ring_send, ring_recv, keys, vals, keys_t, vals_t,
    grad_send, gy_recv, gz_recv, dk_own, dv_own, sums, held, units, invs, k_unit, k_inv,
    cos_ref, sin_ref, gq_t, gk_t, tri, acc_q, part, tot, dp_recv, cp_recv,
    small_sem, in_sem, kvs_sem, kvr_sem, qgs_sem, qgr_sem, ids_sem, idr_sem,
    rs_sem, rr_sem, gys_sem, gyr_sem, gzs_sem, gzr_sem, ds_sem, dr_sem, cs_sem, cr_sem,
):
    a = lax.axis_index("dp")
    c = lax.axis_index("cp")
    reach = min(MOST_BLK - 1, n_cp - 1)
    blocks = reach + 1
    per = grp // pair
    shares = kv * per
    early = min(2, kv)
    ahead = min(3, shares)
    span = pair * d
    even = lax.rem(c, 2) == 0
    even_f = even.astype(F32)
    mate = c + 1 - 2 * lax.rem(c, 2)
    width = grp * d
    rows = tok // n_dp
    inv_root = 1.0 / math.sqrt(d)

    def columns(h, size):
        return pl.ds(pl.multiple_of(h * size, size), size)

    def in_copy(h, src, dst, which):
        return pltpu.make_async_copy(
            src.at[:, columns(h, width)], dst.at[:, columns(h, width)], in_sem.at[2 + which, h]
        )

    k_copy = pltpu.make_async_copy(k_hbm, k_in, in_sem.at[0, 0])
    v_copy = pltpu.make_async_copy(v_hbm, v_in, in_sem.at[1, 0])
    small = [
        pltpu.make_async_copy(src, dst, small_sem.at[i])
        for i, (src, dst) in enumerate(
            [(order_hbm, order_ref), (gq_hbm, gq_ref), (gk_hbm, gk_ref), (table_hbm, table_ref)]
        )
    ]
    small[0].start()
    k_copy.start()
    v_copy.start()
    for copy in small[1:]:
        copy.start()
    for h in range(kv):
        in_copy(h, q_hbm, q_in, 0).start()
        in_copy(h, g_hbm, g_in, 1).start()

    barrier = pltpu.get_barrier_semaphore()
    for r in range(1, n_dp):
        pl.semaphore_signal(
            barrier, inc=1, device_id={"dp": lax.rem(a + r, n_dp)}, device_id_type=MESH
        )

    def greet(r, carry):
        pl.semaphore_signal(
            barrier, inc=1, device_id={"cp": lax.rem(c + r, n_cp)}, device_id_type=MESH
        )
        return carry

    lax.fori_loop(1, n_cp, greet, 0)

    own_id = jnp.broadcast_to(doc_ref[...], (8, 128))
    id_send[...] = own_id
    small[0].wait()
    order = jnp.broadcast_to(order_ref[...], (tok, tok)).astype(F32).T
    slot = lax.broadcasted_iota(jnp.int32, (tok, tok), 1)
    hot[...] = jnp.where(order == slot.astype(F32), 1.0, 0.0).astype(BF16)
    small[1].wait()
    small[2].wait()
    gq_t[...] = jnp.broadcast_to(gq_ref[...], (d, d)).T
    gk_t[...] = jnp.broadcast_to(gk_ref[...], (d, d)).T
    tri[...] = jnp.where(
        lax.broadcasted_iota(jnp.int32, (tok, tok), 0)
        <= lax.broadcasted_iota(jnp.int32, (tok, tok), 1),
        0.0,
        NEGATIVE,
    )
    acc_q[...] = jnp.zeros_like(acc_q)
    for s in range(1, blocks):

        @pl.when(c < s)
        def _():
            id_recv[s - 1] = jnp.zeros((8, 128), jnp.int32)
            for h in range(kv):
                ring_recv[h, s - 1] = jnp.zeros((tok, 2 * d), BF16)

    blank = jnp.zeros((tok, 2 * d), BF16)
    for slot_of, missing in (
        ((0, 0), mate < 1),
        ((0, 1), mate < 3),
        ((1, 0), (c + 2 >= n_cp) | (c < 2)),
        ((1, 1), c + 2 >= n_cp),
    ):

        @pl.when(missing)
        def _():
            for h in range(kv):
                (gy_recv if slot_of[0] == 0 else gz_recv)[h, slot_of[1]] = blank

    k_copy.wait()
    v_copy.wait()
    kw = kv * d
    kv_send[:, :kw] = dot(hot[...], k_in[...]).astype(BF16)
    kv_send[:, kw:] = dot(hot[...], v_in[...]).astype(BF16)
    mine = pl.ds(pl.multiple_of(a * rows, rows), rows)
    kv_recv[mine, :] = kv_send[mine, :]

    pl.semaphore_wait(barrier, n_dp - 1 + n_cp - 1)

    def kv_copy(r):
        peer = lax.rem(a + r, n_dp)
        return pltpu.make_async_remote_copy(
            src_ref=kv_send.at[pl.ds(pl.multiple_of(peer * rows, rows), rows), :],
            dst_ref=kv_recv.at[mine, :],
            send_sem=kvs_sem.at[r - 1],
            recv_sem=kvr_sem.at[r - 1],
            device_id={"dp": peer},
            device_id_type=MESH,
        )

    def qg_copy(i, r):
        peer = lax.rem(a + r, n_dp)
        return pltpu.make_async_remote_copy(
            src_ref=qg_send.at[i, pl.ds(pl.multiple_of(peer * rows, rows), rows), :],
            dst_ref=qg_recv.at[i, mine, :],
            send_sem=qgs_sem.at[i, r - 1],
            recv_sem=qgr_sem.at[i, r - 1],
            device_id={"dp": peer},
            device_id_type=MESH,
        )

    def id_copy(s):
        return pltpu.make_async_remote_copy(
            src_ref=id_send,
            dst_ref=id_recv.at[s - 1],
            send_sem=ids_sem.at[s - 1],
            recv_sem=idr_sem.at[s - 1],
            device_id={"cp": lax.rem(c + s, n_cp)},
            device_id_type=MESH,
        )

    def ring_copy(h, src, to, s, kind):
        return pltpu.make_async_remote_copy(
            src_ref=src,
            dst_ref=ring_recv.at[h, s - 1],
            send_sem=rs_sem.at[h, kind],
            recv_sem=rr_sem.at[h, s - 1],
            device_id={"cp": to},
            device_id_type=MESH,
        )

    behind = lax.rem(c + 2, n_cp)
    front = lax.rem(c + n_cp - 2, n_cp)

    def ring_plan(h):
        own, two, four = ring_send.at[h], ring_recv.at[h, 1], ring_recv.at[h, 3]
        return (
            (ring_copy(h, own, behind, 2, 0), c + 2 < n_cp),
            (ring_copy(h, own, mate, 1, 2), even),
            (ring_copy(h, two, behind, 4, 1), (c >= 2) & (c + 2 < n_cp)),
            (ring_copy(h, two, mate, 3, 3), even & (c >= 2)),
            (ring_copy(h, two, mate, 1, 2), jnp.logical_not(even) & (c >= 2)),
            (ring_copy(h, four, mate, 3, 3), jnp.logical_not(even) & (c >= 4)),
        )

    def ring_arrived(h, s):
        @pl.when(c >= s)
        def _():
            ring_copy(h, ring_send.at[h], mate, s, 0).wait_recv()

    def start_if(plan):
        copy, wanted = plan

        @pl.when(wanted)
        def _():
            copy.start()

    def ring_begin(h):
        for plan in ring_plan(h)[:2]:
            start_if(plan)

    def ring_pass(h):
        ring_arrived(h, 2)
        for plan in ring_plan(h)[2:5]:
            start_if(plan)

    def ring_end(h):
        ring_arrived(h, 4)
        start_if(ring_plan(h)[5])

    def mate_copy(h, i):
        return pltpu.make_async_remote_copy(
            src_ref=grad_send.at[h, 2 * i],
            dst_ref=gy_recv.at[h, i],
            send_sem=gys_sem.at[h, i],
            recv_sem=gyr_sem.at[h, i],
            device_id={"cp": mate},
            device_id_type=MESH,
        )

    def front_copy(h, i):
        return pltpu.make_async_remote_copy(
            src_ref=grad_send.at[h, 3 - 2 * i],
            dst_ref=gz_recv.at[h, i],
            send_sem=gzs_sem.at[h, i],
            recv_sem=gzr_sem.at[h, i],
            device_id={"cp": front},
            device_id_type=MESH,
        )

    def after_mate(h):
        for i in range(2):

            @pl.when(mate >= 1 + 2 * i)
            def _():
                mate_copy(h, i).wait_recv()

        one = gy_recv[h, 0].astype(F32)
        three = gy_recv[h, 1].astype(F32)
        sums[h, 0] = sums[h, 0] + one * even_f
        sums[h, 1] = sums[h, 1] + three * even_f + one * (1.0 - even_f)
        grad_send[h, 3] = (sums[h, 2] + three * (1.0 - even_f)).astype(BF16)

        @pl.when(c >= 4)
        def _():
            front_copy(h, 0).start()

    def after_four(h):
        @pl.when((c + 2 < n_cp) & (c >= 2))
        def _():
            front_copy(h, 0).wait_recv()

        grad_send[h, 1] = (sums[h, 1] + gz_recv[h, 0].astype(F32)).astype(BF16)

        @pl.when(c >= 2)
        def _():
            front_copy(h, 1).start()

    for r in range(1, n_dp):
        kv_copy(r).start()
    for s in range(1, blocks):

        @pl.when(c + s < n_cp)
        def _():
            id_copy(s).start()

    def send_share(i):
        for r in range(1, n_dp):
            qg_copy(i, r).start()

    def gather(i, carry):
        @pl.when(lax.rem(i, per) == 0)
        def _():
            in_copy(i // per, q_hbm, q_in, 0).wait()
            in_copy(i // per, g_hbm, g_in, 1).wait()

        qg_send[i, :, :span] = dot(hot[...], q_in[:, columns(i, span)]).astype(BF16)
        qg_send[i, :, span:] = dot(hot[...], g_in[:, columns(i, span)]).astype(BF16)
        qg_recv[i, mine, :] = qg_send[i, mine, :]

        @pl.when(i == 0)
        def _():
            send_share(0)

        return carry

    lax.fori_loop(0, shares, gather, 0)

    for s in range(1, blocks):

        @pl.when(c >= s)
        def _():
            id_copy(s).wait_recv()

    before = jnp.zeros((1, 128), F32)
    away = []
    for s in range(1, blocks):
        here = (c >= s).astype(F32)
        same = jnp.where(id_recv[s - 1, 0:1, :] == own_id[0:1, :], here, 0.0)
        before = before + same
        away.append(wide((1.0 - same) * -NEGATIVE, pair))
    small[3].wait()
    half = d // 2
    cos = jnp.zeros((half, tok), F32)
    sin = jnp.zeros((half, tok), F32)
    for s in range(MOST_BLK):
        hit = before == float(s)
        cos = cos + jnp.where(hit, table_ref[:half, s * tok : (s + 1) * tok], 0.0)
        sin = sin + jnp.where(hit, table_ref[half:, s * tok : (s + 1) * tok], 0.0)
    cos_ref[...] = cos
    sin_ref[...] = sin

    for r in range(1, n_dp):
        kv_copy(r).wait_recv()
    if ahead > 1:
        send_share(1)

    for h in range(kv):
        x = kv_recv[:, h * d : (h + 1) * d].astype(F32).T
        unit, inv = unit_of(x)
        k_unit[h] = unit
        k_inv[h] = jnp.broadcast_to(inv, (8, tok))
        turned = rotate(unit * gk_t[...], cos_ref[...], sin_ref[...])
        ring_send[h, :, :d] = turned.T.astype(BF16)
        ring_send[h, :, d:] = kv_recv[:, kw + h * d : kw + (h + 1) * d]
        if h < early:
            ring_begin(h)
    for h in range(early):
        ring_pass(h)
    for i in range(2, ahead):
        send_share(i)
    for h in range(early, kv):
        ring_begin(h)
    for h in range(early):
        ring_end(h)

    def head(h, carry):
        ring_arrived(h, 1)
        ring_arrived(h, 3)
        for s in range(blocks):
            both = ring_send[h] if s == 0 else ring_recv[h, s - 1]
            keys[s * tok : (s + 1) * tok, :] = both[:, :d]
            vals[s * tok : (s + 1) * tok, :] = both[:, d:]
            keys_t[:, s * tok : (s + 1) * tok] = both[:, :d].T
            vals_t[:, s * tok : (s + 1) * tok] = both[:, d:].T
        dk_own[...] = jnp.zeros_like(dk_own)
        dv_own[...] = jnp.zeros_like(dv_own)

        def some(j, carry):
            i = h * per + j
            for r in range(1, n_dp):
                qg_copy(i, r).wait_recv()

            @pl.when(i + ahead < shares)
            def _():
                send_share(i + ahead)

            @pl.when(i == 1)
            def _():
                for later in range(early, kv):
                    ring_pass(later)

            cos = wide(cos_ref[...], pair)
            sin = wide(sin_ref[...], pair)
            gain = wide(gq_t[...], pair)
            unit, inv = unit_of(flip(qg_recv[i, :, :span], d).astype(F32))
            units[j] = unit
            invs[j] = jnp.broadcast_to(inv, (8, span))
            turned = rotate(unit * gain, cos, sin).astype(BF16)
            g_rows = qg_recv[i, :, span:]
            g_t = flip(g_rows, d)
            g_rows = jnp.concatenate(
                [g_rows[:, at : at + d] for at in range(0, span, d)], axis=0
            )
            scores = dot(keys[...], turned)
            parts = [scores[s * tok : (s + 1) * tok] for s in range(blocks)]
            parts[0] = parts[0] + wide(tri[...], pair)
            top = jnp.max(parts[0], axis=0, keepdims=True)
            for s in range(1, blocks):
                top = jnp.maximum(top, jnp.max(parts[s], axis=0, keepdims=True) - away[s - 1])
            weights = [
                jnp.exp((parts[s] - (top if s == 0 else top + away[s - 1])) * inv_root)
                for s in range(blocks)
            ]
            weights = jnp.concatenate(weights, axis=0)
            inv_sum = 1.0 / jnp.sum(weights, axis=0, keepdims=True)
            out_t = (dot(vals_t[...], weights.astype(BF16)) * inv_sum).astype(BF16)
            delta = jnp.sum(g_t.astype(F32) * out_t.astype(F32), axis=0, keepdims=True)
            probs = weights * inv_sum
            dprobs = dot(vals[...], g_t)
            dscores = (probs * (dprobs - delta)).astype(BF16)
            dk_own[...] += dot_nt(dscores, turned)
            dv_own[...] += dot(probs.astype(BF16), g_rows)
            held[j] = dscores
            out_buf[:, columns(i, span)] = flip(out_t, d)
            return carry

        lax.fori_loop(0, per, some, 0)
        for s in range(blocks):
            at = slice(s * tok, (s + 1) * tok)
            if s % 2 == 1:
                grad_send[h, s - 1, :, :d] = (dk_own[at, :] * inv_root).astype(BF16)
                grad_send[h, s - 1, :, d:] = dv_own[at, :].astype(BF16)

                @pl.when(c >= s)
                def _():
                    mate_copy(h, s // 2).start()

            else:
                sums[h, s // 2, :, :d] = dk_own[at, :] * inv_root
                sums[h, s // 2, :, d:] = dv_own[at, :]

        @pl.when(h == 0)
        def _():
            for later in range(early, kv):
                ring_end(later)

        def query_grads(j, carry):
            cos = wide(cos_ref[...], pair)
            sin = wide(sin_ref[...], pair)
            unit = units[j]
            dqn = unrotate(dot(keys_t[...], held[j]) * inv_root, cos, sin)
            term = dqn * unit
            acc_q[...] += sum(term[:, at : at + d] for at in range(0, span, d))
            grads = norm_back(dqn, unit, invs[j, 0:1, :], wide(gq_t[...], pair))
            dq_buf[:, columns(h * per + j, span)] = flip(grads.astype(BF16), d)
            return carry

        lax.fori_loop(0, per, query_grads, 0)

        @pl.when(h >= 1)
        def _():
            after_mate(h - 1)

        @pl.when(h >= 2)
        def _():
            after_four(h - 2)

        return carry

    lax.fori_loop(0, kv, head, 0)
    after_mate(kv - 1)
    if kv >= 2:
        after_four(kv - 2)
    acc_k = jnp.zeros((d, tok), F32)
    for h in range(kv):
        if h == max(kv - 2, 0):
            after_four(kv - 1)

        @pl.when(c + 2 < n_cp)
        def _():
            front_copy(h, 1).wait_recv()

        both = sums[h, 0] + gz_recv[h, 1].astype(F32)
        dk, dv = both[:, :d], both[:, d:]
        at = slice(h * d, (h + 1) * d)
        dv_ref[:, at] = dv.astype(BF16)
        dkn = unrotate(dk.T, cos_ref[...], sin_ref[...])
        acc_k = acc_k + dkn * k_unit[h]
        dk_ref[:, at] = norm_back(dkn, k_unit[h], k_inv[h, 0:1, :], gk_t[...]).T.astype(BF16)

    part[...] = jnp.concatenate(
        [
            jnp.sum(acc_q[...].T, axis=0, keepdims=True),
            jnp.sum(acc_k.T, axis=0, keepdims=True),
            jnp.zeros((6, d), F32),
        ],
        axis=0,
    )
    dp_recv[a] = part[...]

    def dp_copy(r):
        return pltpu.make_async_remote_copy(
            src_ref=part,
            dst_ref=dp_recv.at[a],
            send_sem=ds_sem.at[r - 1],
            recv_sem=dr_sem.at[r - 1],
            device_id={"dp": lax.rem(a + r, n_dp)},
            device_id_type=MESH,
        )

    def cp_copy(r):
        return pltpu.make_async_remote_copy(
            src_ref=tot,
            dst_ref=cp_recv.at[c],
            send_sem=cs_sem.at[r - 1],
            recv_sem=cr_sem.at[r - 1],
            device_id={"cp": lax.rem(c + r, n_cp)},
            device_id_type=MESH,
        )

    for r in range(1, n_dp):
        dp_copy(r).start()
    for r in range(1, n_dp):
        dp_copy(r).wait_recv()
    total = dp_recv[0]
    for r in range(1, n_dp):
        total = total + dp_recv[r]
    tot[...] = total
    cp_recv[c] = total

    def each(act):
        def step(r, carry):
            act(cp_copy(r))
            return carry

        lax.fori_loop(1, n_cp, step, 0)

    each(lambda copy: copy.start())

    for r in range(1, n_dp):
        kv_copy(r).wait_send()
        dp_copy(r).wait_send()
    for s in range(1, blocks):

        @pl.when(c + s < n_cp)
        def _():
            id_copy(s).wait_send()

    def settle(h, carry):
        for j in range(per):
            for r in range(1, n_dp):
                qg_copy(h * per + j, r).wait_send()
        for copy, wanted in ring_plan(h):

            @pl.when(wanted)
            def _():
                copy.wait_send()

        for i in range(2):

            @pl.when(c >= 1 + 2 * i)
            def _():
                mate_copy(h, i).wait_send()

            @pl.when(c >= 4 - 2 * i)
            def _():
                front_copy(h, i).wait_send()

        return carry

    lax.fori_loop(0, kv, settle, 0)
    each(lambda copy: copy.wait())
    total = lax.fori_loop(1, n_cp, lambda r, sofar: sofar + cp_recv[r], cp_recv[0])
    total = total * (1.0 / math.sqrt(tok * n_dp * n_cp))
    gains_ref[...] = total


def hand_out(out, dq, dk, dv, gains, out_o, dq_o, dk_o, dv_o, gq_o, gk_o, sem):
    pairs = [
        (out, out_o), (dq, dq_o), (dk, dk_o), (dv, dv_o),
        (gains.at[0:1], gq_o), (gains.at[1:2], gk_o),
    ]
    copies = [pltpu.make_async_copy(src, dst, sem.at[i]) for i, (src, dst) in enumerate(pairs)]
    for copy in copies:
        copy.start()
    for copy in copies:
        copy.wait()


def body(n_dp, n_cp, q_raw, k_raw, values, loss_grad, send_order, doc_blocks, gain_q, gain_k):
    tok, q_width = q_raw.shape
    kw = k_raw.shape[1]
    d = gain_q.shape[0]
    kv = kw // d
    grp = q_width // kw
    blocks = min(MOST_BLK, n_cp)
    reach = blocks - 1
    pair = 4 if grp % 8 == 0 else 1
    per = grp // pair
    assert doc_blocks.shape == (1, 1) and n_cp % 2 == 0 and n_cp >= 6 and MOST_BLK == 5
    frequency = THETA ** (-(np.arange(d // 2, dtype=np.float64) * 2.0 / d))
    angles = frequency[:, None] * np.arange(MOST_BLK * tok, dtype=np.float64)[None, :]
    table = jnp.asarray(np.concatenate([np.cos(angles), np.sin(angles)]).astype(np.float32))
    vmem = pl.BlockSpec(memory_space=pltpu.VMEM)
    hbm = pl.BlockSpec(memory_space=pltpu.HBM)
    dma = pltpu.SemaphoreType.DMA
    V = pltpu.VMEM
    outs = pl.pallas_call(
        functools.partial(kernel, n_dp, n_cp, kv, grp, d, tok, pair),
        out_shape=[
            V((tok, q_width), BF16),
            V((tok, q_width), BF16),
            V((tok, kw), BF16),
            V((tok, kw), BF16),
            V((8, d), F32),
        ],
        in_specs=[hbm] * 5 + [vmem] + [hbm] * 3,
        out_specs=[vmem] * 5,
        scratch_shapes=[
            V((tok, q_width), BF16),
            V((tok, kw), BF16),
            V((tok, kw), BF16),
            V((tok, q_width), BF16),
            V((1, tok), jnp.int32),
            V((1, d), F32),
            V((1, d), F32),
            V(table.shape, F32),
            V((tok, tok), BF16),
            V((tok, 2 * kw), BF16),
            V((tok, 2 * kw), BF16),
            V((kv * per, tok, 2 * pair * d), BF16),
            V((kv * per, tok, 2 * pair * d), BF16),
            V((8, 128), jnp.int32),
            V((reach, 8, 128), jnp.int32),
            V((kv, tok, 2 * d), BF16),
            V((kv, reach, tok, 2 * d), BF16),
            V((blocks * tok, d), BF16),
            V((blocks * tok, d), BF16),
            V((d, blocks * tok), BF16),
            V((d, blocks * tok), BF16),
            V((kv, reach, tok, 2 * d), BF16),
            V((kv, 2, tok, 2 * d), BF16),
            V((kv, 2, tok, 2 * d), BF16),
            V((blocks * tok, d), F32),
            V((blocks * tok, d), F32),
            V((kv, 3, tok, 2 * d), F32),
            V((per, blocks * tok, pair * d), BF16),
            V((per, d, pair * d), F32),
            V((per, 8, pair * d), F32),
            V((kv, d, tok), F32),
            V((kv, 8, tok), F32),
            V((d // 2, tok), F32),
            V((d // 2, tok), F32),
            V((d, d), F32),
            V((d, d), F32),
            V((tok, tok), F32),
            V((d, tok), F32),
            V((8, d), F32),
            V((8, d), F32),
            V((n_dp, 8, d), F32),
            V((n_cp, 8, d), F32),
            dma((4,)),
            dma((4, kv)),
            dma((n_dp - 1,)),
            dma((n_dp - 1,)),
            dma((kv * per, n_dp - 1)),
            dma((kv * per, n_dp - 1)),
            dma((reach,)),
            dma((reach,)),
            dma((kv, 4)),
            dma((kv, reach)),
            dma((kv, 2)),
            dma((kv, 2)),
            dma((kv, 2)),
            dma((kv, 2)),
            dma((n_dp - 1,)),
            dma((n_dp - 1,)),
            dma((n_cp - 1,)),
            dma((n_cp - 1,)),
        ],
        compiler_params=pltpu.CompilerParams(
            collective_id=0, has_side_effects=True, vmem_limit_bytes=56 * 1024 * 1024
        ),
    )(
        q_raw, k_raw, values, loss_grad, send_order, doc_blocks,
        gain_q.reshape(1, d), gain_k.reshape(1, d), table,
    )
    outs = pl.pallas_call(
        hand_out,
        out_shape=[jax.ShapeDtypeStruct(x.shape, x.dtype) for x in outs[:4]]
        + [jax.ShapeDtypeStruct((1, d), F32)] * 2,
        in_specs=[vmem] * 5,
        out_specs=[hbm] * 6,
        scratch_shapes=[dma((6,))],
        compiler_params=pltpu.CompilerParams(vmem_limit_bytes=8 * 1024 * 1024),
    )(*outs)
    return (*outs[:4], outs[4].reshape(d), outs[5].reshape(d))


def solution(mesh):
    split = P(("dp", "cp"), None)
    return jax.shard_map(
        functools.partial(body, mesh.shape["dp"], mesh.shape["cp"]),
        mesh=mesh,
        in_specs=(split,) * 5 + (P("dp", "cp"), P(), P()),
        out_specs=(split,) * 4 + (P(), P()),
        check_vma=False,
    )
```

```python
import functools
import math

import jax
import jax.numpy as jnp
import numpy as np
from jax import lax
from jax.experimental import pallas as pl
from jax.experimental.pallas import tpu as pltpu
from jax.sharding import PartitionSpec as P

MOST_BLK = 5
EPSILON = 1e-06
THETA = 1000000.0
NEGATIVE = -1e30
MESH = pl.DeviceIdType.MESH
F32 = jnp.float32
BF16 = jnp.bfloat16


def dot(a, b):
    return jnp.dot(a, b, preferred_element_type=F32)


def dot_nt(a, b):
    return lax.dot_general(a, b, (((1,), (1,)), ((), ())), preferred_element_type=F32)


def flip(x, d):
    parts = [x[:, i : i + d].T for i in range(0, x.shape[1], d)]
    return parts[0] if len(parts) == 1 else jnp.concatenate(parts, axis=1)


def wide(x, n):
    return x if n == 1 else jnp.concatenate([x] * n, axis=1)


def rotate(x, cos, sin):
    half = x.shape[0] // 2
    lead, trail = x[:half], x[half:]
    return jnp.concatenate([lead * cos - trail * sin, trail * cos + lead * sin], axis=0)


def unrotate(x, cos, sin):
    half = x.shape[0] // 2
    lead, trail = x[:half], x[half:]
    return jnp.concatenate([lead * cos + trail * sin, trail * cos - lead * sin], axis=0)


def unit_of(x):
    inv = lax.rsqrt(jnp.mean(x * x, axis=0, keepdims=True) + EPSILON)
    return x * inv, inv


def norm_back(cot, unit, inv, gain):
    scaled = cot * gain
    inner = jnp.mean(scaled * unit, axis=0, keepdims=True)
    return inv * (scaled - unit * inner)


def kernel(
    n_dp, n_cp, kv, grp, d, tok, pair,
    q_hbm, k_hbm, v_hbm, g_hbm, order_hbm, doc_ref, gq_hbm, gk_hbm, table_hbm,
    out_buf, dq_buf, dk_ref, dv_ref, gains_ref,
    q_in, k_in, v_in, g_in, order_ref, gq_ref, gk_ref, table_ref, hot, kv_send, kv_recv, qg_send, qg_recv,
    id_send, id_recv, ring_send, ring_recv, keys, vals, keys_t, vals_t,
    grad_send, gy_recv, gz_recv, dk_own, dv_own, sums, held, units, invs, k_unit, k_inv,
    cos_ref, sin_ref, gq_t, gk_t, tri, acc_q, part, tot, dp_recv, cp_recv,
    small_sem, in_sem, kvs_sem, kvr_sem, qgs_sem, qgr_sem, ids_sem, idr_sem,
    rs_sem, rr_sem, gys_sem, gyr_sem, gzs_sem, gzr_sem, ds_sem, dr_sem, cs_sem, cr_sem,
):
    a = lax.axis_index("dp")
    c = lax.axis_index("cp")
    reach = min(MOST_BLK - 1, n_cp - 1)
    blocks = reach + 1
    per = grp // pair
    shares = kv * per
    early = min(2, kv)
    ahead = min(5, shares)
    span = pair * d
    even = lax.rem(c, 2) == 0
    even_f = even.astype(F32)
    mate = c + 1 - 2 * lax.rem(c, 2)
    width = grp * d
    rows = tok // n_dp
    inv_root = 1.0 / math.sqrt(d)

    def columns(h, size):
        return pl.ds(pl.multiple_of(h * size, size), size)

    def in_copy(h, src, dst, which):
        return pltpu.make_async_copy(
            src.at[:, columns(h, width)], dst.at[:, columns(h, width)], in_sem.at[2 + which, h]
        )

    k_copy = pltpu.make_async_copy(k_hbm, k_in, in_sem.at[0, 0])
    v_copy = pltpu.make_async_copy(v_hbm, v_in, in_sem.at[1, 0])
    small = [
        pltpu.make_async_copy(src, dst, small_sem.at[i])
        for i, (src, dst) in enumerate(
            [(order_hbm, order_ref), (gq_hbm, gq_ref), (gk_hbm, gk_ref), (table_hbm, table_ref)]
        )
    ]
    small[0].start()
    k_copy.start()
    v_copy.start()
    for copy in small[1:]:
        copy.start()
    for h in range(kv):
        in_copy(h, q_hbm, q_in, 0).start()
        in_copy(h, g_hbm, g_in, 1).start()

    barrier = pltpu.get_barrier_semaphore()
    for r in range(1, n_dp):
        pl.semaphore_signal(
            barrier, inc=1, device_id={"dp": lax.rem(a + r, n_dp)}, device_id_type=MESH
        )

    def greet(r, carry):
        pl.semaphore_signal(
            barrier, inc=1, device_id={"cp": lax.rem(c + r, n_cp)}, device_id_type=MESH
        )
        return carry

    lax.fori_loop(1, n_cp, greet, 0)

    own_id = jnp.broadcast_to(doc_ref[...], (8, 128))
    id_send[...] = own_id
    small[0].wait()
    order = jnp.broadcast_to(order_ref[...], (tok, tok)).astype(F32).T
    slot = lax.broadcasted_iota(jnp.int32, (tok, tok), 1)
    hot[...] = jnp.where(order == slot.astype(F32), 1.0, 0.0).astype(BF16)
    small[1].wait()
    small[2].wait()
    gq_t[...] = jnp.broadcast_to(gq_ref[...], (d, d)).T
    gk_t[...] = jnp.broadcast_to(gk_ref[...], (d, d)).T
    tri[...] = jnp.where(
        lax.broadcasted_iota(jnp.int32, (tok, tok), 0)
        <= lax.broadcasted_iota(jnp.int32, (tok, tok), 1),
        0.0,
        NEGATIVE,
    )
    acc_q[...] = jnp.zeros_like(acc_q)
    for s in range(1, blocks):

        @pl.when(c < s)
        def _():
            id_recv[s - 1] = jnp.zeros((8, 128), jnp.int32)
            for h in range(kv):
                ring_recv[h, s - 1] = jnp.zeros((tok, 2 * d), BF16)

    blank = jnp.zeros((tok, 2 * d), BF16)
    for slot_of, missing in (
        ((0, 0), mate < 1),
        ((0, 1), mate < 3),
        ((1, 0), (c + 2 >= n_cp) | (c < 2)),
        ((1, 1), c + 2 >= n_cp),
    ):

        @pl.when(missing)
        def _():
            for h in range(kv):
                (gy_recv if slot_of[0] == 0 else gz_recv)[h, slot_of[1]] = blank

    k_copy.wait()
    v_copy.wait()
    kw = kv * d
    kv_send[:, :kw] = dot(hot[...], k_in[...]).astype(BF16)
    kv_send[:, kw:] = dot(hot[...], v_in[...]).astype(BF16)
    mine = pl.ds(pl.multiple_of(a * rows, rows), rows)
    kv_recv[mine, :] = kv_send[mine, :]

    pl.semaphore_wait(barrier, n_dp - 1 + n_cp - 1)

    def kv_copy(r):
        peer = lax.rem(a + r, n_dp)
        return pltpu.make_async_remote_copy(
            src_ref=kv_send.at[pl.ds(pl.multiple_of(peer * rows, rows), rows), :],
            dst_ref=kv_recv.at[mine, :],
            send_sem=kvs_sem.at[r - 1],
            recv_sem=kvr_sem.at[r - 1],
            device_id={"dp": peer},
            device_id_type=MESH,
        )

    def qg_copy(i, r):
        peer = lax.rem(a + r, n_dp)
        return pltpu.make_async_remote_copy(
            src_ref=qg_send.at[i, pl.ds(pl.multiple_of(peer * rows, rows), rows), :],
            dst_ref=qg_recv.at[i, mine, :],
            send_sem=qgs_sem.at[i, r - 1],
            recv_sem=qgr_sem.at[i, r - 1],
            device_id={"dp": peer},
            device_id_type=MESH,
        )

    def id_copy(s):
        return pltpu.make_async_remote_copy(
            src_ref=id_send,
            dst_ref=id_recv.at[s - 1],
            send_sem=ids_sem.at[s - 1],
            recv_sem=idr_sem.at[s - 1],
            device_id={"cp": lax.rem(c + s, n_cp)},
            device_id_type=MESH,
        )

    def ring_copy(h, src, to, s, kind):
        return pltpu.make_async_remote_copy(
            src_ref=src,
            dst_ref=ring_recv.at[h, s - 1],
            send_sem=rs_sem.at[h, kind],
            recv_sem=rr_sem.at[h, s - 1],
            device_id={"cp": to},
            device_id_type=MESH,
        )

    behind = lax.rem(c + 2, n_cp)
    front = lax.rem(c + n_cp - 2, n_cp)

    def ring_plan(h):
        own, two, four = ring_send.at[h], ring_recv.at[h, 1], ring_recv.at[h, 3]
        return (
            (ring_copy(h, own, behind, 2, 0), c + 2 < n_cp),
            (ring_copy(h, own, mate, 1, 2), even),
            (ring_copy(h, two, behind, 4, 1), (c >= 2) & (c + 2 < n_cp)),
            (ring_copy(h, two, mate, 3, 3), even & (c >= 2)),
            (ring_copy(h, two, mate, 1, 2), jnp.logical_not(even) & (c >= 2)),
            (ring_copy(h, four, mate, 3, 3), jnp.logical_not(even) & (c >= 4)),
        )

    def ring_arrived(h, s):
        @pl.when(c >= s)
        def _():
            ring_copy(h, ring_send.at[h], mate, s, 0).wait_recv()

    def start_if(plan):
        copy, wanted = plan

        @pl.when(wanted)
        def _():
            copy.start()

    def ring_begin(h):
        for plan in ring_plan(h)[:2]:
            start_if(plan)

    def ring_pass(h):
        ring_arrived(h, 2)
        for plan in ring_plan(h)[2:5]:
            start_if(plan)

    def ring_end(h):
        ring_arrived(h, 4)
        start_if(ring_plan(h)[5])

    halves = (slice(0, d), slice(d, 2 * d))

    def mate_copy(h, i, p):
        return pltpu.make_async_remote_copy(
            src_ref=grad_send.at[h, 2 * i, :, pl.ds(p * d, d)],
            dst_ref=gy_recv.at[h, i, :, pl.ds(p * d, d)],
            send_sem=gys_sem.at[h, i, p],
            recv_sem=gyr_sem.at[h, i, p],
            device_id={"cp": mate},
            device_id_type=MESH,
        )

    def front_copy(h, i, p):
        return pltpu.make_async_remote_copy(
            src_ref=grad_send.at[h, 3 - 2 * i, :, pl.ds(p * d, d)],
            dst_ref=gz_recv.at[h, i, :, pl.ds(p * d, d)],
            send_sem=gzs_sem.at[h, i, p],
            recv_sem=gzr_sem.at[h, i, p],
            device_id={"cp": front},
            device_id_type=MESH,
        )

    def after_mate(h):
        for p, at in enumerate(halves):
            for i in range(2):

                @pl.when(mate >= 1 + 2 * i)
                def _():
                    mate_copy(h, i, p).wait_recv()

            one = gy_recv[h, 0, :, at].astype(F32)
            three = gy_recv[h, 1, :, at].astype(F32)
            last = sums[h, 2, :, at] + three * (1.0 - even_f)
            grad_send[h, 3, :, at] = last.astype(BF16)

            @pl.when(c >= 4)
            def _():
                front_copy(h, 0, p).start()

            sums[h, 0, :, at] = sums[h, 0, :, at] + one * even_f
            sums[h, 1, :, at] = sums[h, 1, :, at] + three * even_f + one * (1.0 - even_f)

    def after_four(h):
        for p, at in enumerate(halves):

            @pl.when((c + 2 < n_cp) & (c >= 2))
            def _():
                front_copy(h, 0, p).wait_recv()

            both = sums[h, 1, :, at] + gz_recv[h, 0, :, at].astype(F32)
            grad_send[h, 1, :, at] = both.astype(BF16)

            @pl.when(c >= 2)
            def _():
                front_copy(h, 1, p).start()

    for r in range(1, n_dp):
        kv_copy(r).start()
    for s in range(1, blocks):

        @pl.when(c + s < n_cp)
        def _():
            id_copy(s).start()

    def gather(i, carry):
        @pl.when(lax.rem(i, per) == 0)
        def _():
            in_copy(i // per, q_hbm, q_in, 0).wait()
            in_copy(i // per, g_hbm, g_in, 1).wait()

        qg_send[i, :, :span] = dot(hot[...], q_in[:, columns(i, span)]).astype(BF16)
        qg_send[i, :, span:] = dot(hot[...], g_in[:, columns(i, span)]).astype(BF16)
        qg_recv[i, mine, :] = qg_send[i, mine, :]

        @pl.when(i < ahead)
        def _():
            for r in range(1, n_dp):
                qg_copy(i, r).start()

        return carry

    lax.fori_loop(0, shares, gather, 0)

    for s in range(1, blocks):

        @pl.when(c >= s)
        def _():
            id_copy(s).wait_recv()

    before = jnp.zeros((1, 128), F32)
    away = []
    for s in range(1, blocks):
        here = (c >= s).astype(F32)
        same = jnp.where(id_recv[s - 1, 0:1, :] == own_id[0:1, :], here, 0.0)
        before = before + same
        away.append(wide((1.0 - same) * -NEGATIVE, pair))
    small[3].wait()
    half = d // 2
    cos = jnp.zeros((half, tok), F32)
    sin = jnp.zeros((half, tok), F32)
    for s in range(MOST_BLK):
        hit = before == float(s)
        cos = cos + jnp.where(hit, table_ref[:half, s * tok : (s + 1) * tok], 0.0)
        sin = sin + jnp.where(hit, table_ref[half:, s * tok : (s + 1) * tok], 0.0)
    cos_ref[...] = cos
    sin_ref[...] = sin

    for r in range(1, n_dp):
        kv_copy(r).wait_recv()

    for h in range(kv):
        x = kv_recv[:, h * d : (h + 1) * d].astype(F32).T
        unit, inv = unit_of(x)
        k_unit[h] = unit
        k_inv[h] = jnp.broadcast_to(inv, (8, tok))
        turned = rotate(unit * gk_t[...], cos_ref[...], sin_ref[...])
        ring_send[h, :, :d] = turned.T.astype(BF16)
        ring_send[h, :, d:] = kv_recv[:, kw + h * d : kw + (h + 1) * d]
        if h < early:
            ring_begin(h)
    for h in range(early):
        ring_pass(h)
    for h in range(early, kv):
        ring_begin(h)
    for h in range(early):
        ring_end(h)

    def head(h, carry):
        ring_arrived(h, 1)
        ring_arrived(h, 3)
        for s in range(blocks):
            both = ring_send[h] if s == 0 else ring_recv[h, s - 1]
            keys[s * tok : (s + 1) * tok, :] = both[:, :d]
            vals[s * tok : (s + 1) * tok, :] = both[:, d:]
            keys_t[:, s * tok : (s + 1) * tok] = both[:, :d].T
            vals_t[:, s * tok : (s + 1) * tok] = both[:, d:].T
        dk_own[...] = jnp.zeros_like(dk_own)
        dv_own[...] = jnp.zeros_like(dv_own)

        def some(j, carry):
            i = h * per + j
            for r in range(1, n_dp):
                qg_copy(i, r).wait_recv()

            @pl.when(i + ahead < shares)
            def _():
                for r in range(1, n_dp):
                    qg_copy(i + ahead, r).start()

            @pl.when(i == 1)
            def _():
                for later in range(early, kv):
                    ring_pass(later)

            cos = wide(cos_ref[...], pair)
            sin = wide(sin_ref[...], pair)
            gain = wide(gq_t[...], pair)
            unit, inv = unit_of(flip(qg_recv[i, :, :span], d).astype(F32))
            units[j] = unit
            invs[j] = jnp.broadcast_to(inv, (8, span))
            turned = rotate(unit * gain, cos, sin).astype(BF16)
            g_rows = qg_recv[i, :, span:]
            g_t = flip(g_rows, d)
            g_rows = jnp.concatenate(
                [g_rows[:, at : at + d] for at in range(0, span, d)], axis=0
            )
            scores = dot(keys[...], turned)
            parts = [scores[s * tok : (s + 1) * tok] for s in range(blocks)]
            parts[0] = parts[0] + wide(tri[...], pair)
            top = jnp.max(parts[0], axis=0, keepdims=True)
            for s in range(1, blocks):
                top = jnp.maximum(top, jnp.max(parts[s], axis=0, keepdims=True) - away[s - 1])
            weights = [
                jnp.exp((parts[s] - (top if s == 0 else top + away[s - 1])) * inv_root)
                for s in range(blocks)
            ]
            weights = jnp.concatenate(weights, axis=0)
            inv_sum = 1.0 / jnp.sum(weights, axis=0, keepdims=True)
            out_t = (dot(vals_t[...], weights.astype(BF16)) * inv_sum).astype(BF16)
            delta = jnp.sum(g_t.astype(F32) * out_t.astype(F32), axis=0, keepdims=True)
            probs = weights * inv_sum
            dprobs = dot(vals[...], g_t)
            dscores = (probs * (dprobs - delta)).astype(BF16)
            dk_own[...] += dot_nt(dscores, turned)
            dv_own[...] += dot(probs.astype(BF16), g_rows)
            held[j] = dscores
            out_buf[:, columns(i, span)] = flip(out_t, d)
            return carry

        lax.fori_loop(0, per, some, 0)
        for s in range(blocks):
            at = slice(s * tok, (s + 1) * tok)
            if s % 2 == 1:
                grad_send[h, s - 1, :, :d] = (dk_own[at, :] * inv_root).astype(BF16)
                grad_send[h, s - 1, :, d:] = dv_own[at, :].astype(BF16)
            else:
                sums[h, s // 2, :, :d] = dk_own[at, :] * inv_root
                sums[h, s // 2, :, d:] = dv_own[at, :]
        for p in range(2):
            for i in range(2):

                @pl.when(c >= 1 + 2 * i)
                def _():
                    mate_copy(h, i, p).start()

        @pl.when(h == 0)
        def _():
            for later in range(early, kv):
                ring_end(later)

        def query_grads(j, carry):
            cos = wide(cos_ref[...], pair)
            sin = wide(sin_ref[...], pair)
            unit = units[j]
            dqn = unrotate(dot(keys_t[...], held[j]) * inv_root, cos, sin)
            term = dqn * unit
            acc_q[...] += sum(term[:, at : at + d] for at in range(0, span, d))
            grads = norm_back(dqn, unit, invs[j, 0:1, :], wide(gq_t[...], pair))
            dq_buf[:, columns(h * per + j, span)] = flip(grads.astype(BF16), d)
            return carry

        lax.fori_loop(0, per, query_grads, 0)

        @pl.when(h >= 1)
        def _():
            after_mate(h - 1)

        @pl.when(h >= 2)
        def _():
            after_four(h - 2)

        return carry

    lax.fori_loop(0, kv, head, 0)
    after_mate(kv - 1)
    if kv >= 2:
        after_four(kv - 2)
    acc_k = jnp.zeros((d, tok), F32)
    for h in range(kv):
        if h == max(kv - 2, 0):
            after_four(kv - 1)

        @pl.when(c + 2 < n_cp)
        def _():
            for p in range(2):
                front_copy(h, 1, p).wait_recv()

        both = sums[h, 0] + gz_recv[h, 1].astype(F32)
        dk, dv = both[:, :d], both[:, d:]
        at = slice(h * d, (h + 1) * d)
        dv_ref[:, at] = dv.astype(BF16)
        dkn = unrotate(dk.T, cos_ref[...], sin_ref[...])
        acc_k = acc_k + dkn * k_unit[h]
        dk_ref[:, at] = norm_back(dkn, k_unit[h], k_inv[h, 0:1, :], gk_t[...]).T.astype(BF16)

    part[...] = jnp.concatenate(
        [
            jnp.sum(acc_q[...].T, axis=0, keepdims=True),
            jnp.sum(acc_k.T, axis=0, keepdims=True),
            jnp.zeros((6, d), F32),
        ],
        axis=0,
    )
    dp_recv[a] = part[...]

    def dp_copy(r):
        return pltpu.make_async_remote_copy(
            src_ref=part,
            dst_ref=dp_recv.at[a],
            send_sem=ds_sem.at[r - 1],
            recv_sem=dr_sem.at[r - 1],
            device_id={"dp": lax.rem(a + r, n_dp)},
            device_id_type=MESH,
        )

    def cp_copy(r):
        return pltpu.make_async_remote_copy(
            src_ref=tot,
            dst_ref=cp_recv.at[c],
            send_sem=cs_sem.at[r - 1],
            recv_sem=cr_sem.at[r - 1],
            device_id={"cp": lax.rem(c + r, n_cp)},
            device_id_type=MESH,
        )

    for r in range(1, n_dp):
        dp_copy(r).start()
    for r in range(1, n_dp):
        dp_copy(r).wait_recv()
    total = dp_recv[0]
    for r in range(1, n_dp):
        total = total + dp_recv[r]
    tot[...] = total
    cp_recv[c] = total

    def each(act):
        def step(r, carry):
            act(cp_copy(r))
            return carry

        lax.fori_loop(1, n_cp, step, 0)

    each(lambda copy: copy.start())

    for r in range(1, n_dp):
        kv_copy(r).wait_send()
        dp_copy(r).wait_send()
    for s in range(1, blocks):

        @pl.when(c + s < n_cp)
        def _():
            id_copy(s).wait_send()

    def settle(h, carry):
        for j in range(per):
            for r in range(1, n_dp):
                qg_copy(h * per + j, r).wait_send()
        for copy, wanted in ring_plan(h):

            @pl.when(wanted)
            def _():
                copy.wait_send()

        for i in range(2):

            @pl.when(c >= 1 + 2 * i)
            def _():
                for p in range(2):
                    mate_copy(h, i, p).wait_send()

            @pl.when(c >= 4 - 2 * i)
            def _():
                for p in range(2):
                    front_copy(h, i, p).wait_send()

        return carry

    lax.fori_loop(0, kv, settle, 0)
    each(lambda copy: copy.wait())
    total = lax.fori_loop(1, n_cp, lambda r, sofar: sofar + cp_recv[r], cp_recv[0])
    total = total * (1.0 / math.sqrt(tok * n_dp * n_cp))
    gains_ref[...] = total


def hand_out(out, dq, dk, dv, gains, out_o, dq_o, dk_o, dv_o, gq_o, gk_o, sem):
    pairs = [
        (out, out_o), (dq, dq_o), (dk, dk_o), (dv, dv_o),
        (gains.at[0:1], gq_o), (gains.at[1:2], gk_o),
    ]
    copies = [pltpu.make_async_copy(src, dst, sem.at[i]) for i, (src, dst) in enumerate(pairs)]
    for copy in copies:
        copy.start()
    for copy in copies:
        copy.wait()


def body(n_dp, n_cp, q_raw, k_raw, values, loss_grad, send_order, doc_blocks, gain_q, gain_k):
    tok, q_width = q_raw.shape
    kw = k_raw.shape[1]
    d = gain_q.shape[0]
    kv = kw // d
    grp = q_width // kw
    blocks = min(MOST_BLK, n_cp)
    reach = blocks - 1
    pair = 4 if grp % 8 == 0 else 1
    per = grp // pair
    assert doc_blocks.shape == (1, 1) and n_cp % 2 == 0 and n_cp >= 6 and MOST_BLK == 5
    frequency = THETA ** (-(np.arange(d // 2, dtype=np.float64) * 2.0 / d))
    angles = frequency[:, None] * np.arange(MOST_BLK * tok, dtype=np.float64)[None, :]
    table = jnp.asarray(np.concatenate([np.cos(angles), np.sin(angles)]).astype(np.float32))
    vmem = pl.BlockSpec(memory_space=pltpu.VMEM)
    hbm = pl.BlockSpec(memory_space=pltpu.HBM)
    dma = pltpu.SemaphoreType.DMA
    V = pltpu.VMEM
    outs = pl.pallas_call(
        functools.partial(kernel, n_dp, n_cp, kv, grp, d, tok, pair),
        out_shape=[
            V((tok, q_width), BF16),
            V((tok, q_width), BF16),
            V((tok, kw), BF16),
            V((tok, kw), BF16),
            V((8, d), F32),
        ],
        in_specs=[hbm] * 5 + [vmem] + [hbm] * 3,
        out_specs=[vmem] * 5,
        scratch_shapes=[
            V((tok, q_width), BF16),
            V((tok, kw), BF16),
            V((tok, kw), BF16),
            V((tok, q_width), BF16),
            V((1, tok), jnp.int32),
            V((1, d), F32),
            V((1, d), F32),
            V(table.shape, F32),
            V((tok, tok), BF16),
            V((tok, 2 * kw), BF16),
            V((tok, 2 * kw), BF16),
            V((kv * per, tok, 2 * pair * d), BF16),
            V((kv * per, tok, 2 * pair * d), BF16),
            V((8, 128), jnp.int32),
            V((reach, 8, 128), jnp.int32),
            V((kv, tok, 2 * d), BF16),
            V((kv, reach, tok, 2 * d), BF16),
            V((blocks * tok, d), BF16),
            V((blocks * tok, d), BF16),
            V((d, blocks * tok), BF16),
            V((d, blocks * tok), BF16),
            V((kv, reach, tok, 2 * d), BF16),
            V((kv, 2, tok, 2 * d), BF16),
            V((kv, 2, tok, 2 * d), BF16),
            V((blocks * tok, d), F32),
            V((blocks * tok, d), F32),
            V((kv, 3, tok, 2 * d), F32),
            V((per, blocks * tok, pair * d), BF16),
            V((per, d, pair * d), F32),
            V((per, 8, pair * d), F32),
            V((kv, d, tok), F32),
            V((kv, 8, tok), F32),
            V((d // 2, tok), F32),
            V((d // 2, tok), F32),
            V((d, d), F32),
            V((d, d), F32),
            V((tok, tok), F32),
            V((d, tok), F32),
            V((8, d), F32),
            V((8, d), F32),
            V((n_dp, 8, d), F32),
            V((n_cp, 8, d), F32),
            dma((4,)),
            dma((4, kv)),
            dma((n_dp - 1,)),
            dma((n_dp - 1,)),
            dma((kv * per, n_dp - 1)),
            dma((kv * per, n_dp - 1)),
            dma((reach,)),
            dma((reach,)),
            dma((kv, 4)),
            dma((kv, reach)),
            dma((kv, 2, 2)),
            dma((kv, 2, 2)),
            dma((kv, 2, 2)),
            dma((kv, 2, 2)),
            dma((n_dp - 1,)),
            dma((n_dp - 1,)),
            dma((n_cp - 1,)),
            dma((n_cp - 1,)),
        ],
        compiler_params=pltpu.CompilerParams(
            collective_id=0, has_side_effects=True, vmem_limit_bytes=56 * 1024 * 1024
        ),
    )(
        q_raw, k_raw, values, loss_grad, send_order, doc_blocks,
        gain_q.reshape(1, d), gain_k.reshape(1, d), table,
    )
    outs = pl.pallas_call(
        hand_out,
        out_shape=[jax.ShapeDtypeStruct(x.shape, x.dtype) for x in outs[:4]]
        + [jax.ShapeDtypeStruct((1, d), F32)] * 2,
        in_specs=[vmem] * 5,
        out_specs=[hbm] * 6,
        scratch_shapes=[dma((6,))],
        compiler_params=pltpu.CompilerParams(vmem_limit_bytes=8 * 1024 * 1024),
    )(*outs)
    return (*outs[:4], outs[4].reshape(d), outs[5].reshape(d))


def solution(mesh):
    split = P(("dp", "cp"), None)
    return jax.shard_map(
        functools.partial(body, mesh.shape["dp"], mesh.shape["cp"]),
        mesh=mesh,
        in_specs=(split,) * 5 + (P("dp", "cp"), P(), P()),
        out_specs=(split,) * 4 + (P(), P()),
        check_vma=False,
    )
```
